128 devices in a mesh: seq: 32 (over x, y, core), kv: 4 (over z).
Axes of the slice: x: 4, y: 4, z: 4, core: 2. Of those that a mesh axis runs over, the one named last changes fastest.
Arguments:
- queries: bfloat16 [8192, 4096], P('seq', 'kv'), as said below
- keys: bfloat16 [8192, 1024], P('seq', 'kv'), as said below
- values: bfloat16 [8192, 1024], P('seq', 'kv'), may hold values from -6 to 6
- out_weight: bfloat16 [4096, 4096], P(None, 'kv'), may hold values from -0.09375 to 0.09375
- out_grad: bfloat16 [8192, 4096], P('seq', 'kv'), may hold values from -6 to 6
- doc_lengths: int32 [64], replicated, may hold values from 1 to 768, 8192 in all
Outputs:
- layer_out: bfloat16 [8192, 4096], P('seq', 'kv')
- query_grad: bfloat16 [8192, 4096], P('seq', 'kv')
- key_grad: bfloat16 [8192, 1024], P('seq', 'kv')
- value_grad: bfloat16 [8192, 1024], P('seq', 'kv')
- weight_grad: bfloat16 [4096, 4096], P('seq', 'kv')
The draws below stay inside these ranges and needn't reach their ends.
Inputs may be any that keep to these rules, and one draw needn't show every extreme that they name: `queries`: every entry lies within -8 to 8. `keys`: every entry lies within -8 to 8. `doc_lengths`: the lengths sum to 8192; the longest document has exactly 768 tokens.
All inputs are finite; a program needn't handle non-finite values.
Results may differ from the reference program's by a relative error of at most 0.03.
Values may be sent and summed in bfloat16 or wider, within the bound.
No kernel may reach another device: no remote copies, remote signals or barrier semaphores. Data moves between devices by JAX's collectives and lax.ppermute only.
A program may use at most 128 MiB of HBM per device.

```python
import math
import jax
import jax.numpy as jnp
import numpy as np
from jax import lax

D = 4096
QUERY_HEAD_COUNT = 32
KEY_VALUE_HEADS = 8
HEAD_SIZE = 128
TOK_DEV = 256
REACH = 3
PACKED_TOKENS = 8192
MAXDOC = 768
NDOCS = 64


def draw_queries(key, part):
    key = jax.random.fold_in(key, 11)
    return jnp.clip(jax.random.normal(key, (PACKED_TOKENS, QUERY_HEAD_COUNT * HEAD_SIZE), jnp.float32), -6.0, 6.0).astype(jnp.bfloat16)


def draw_keys(key, part):
    key = jax.random.fold_in(key, 23)
    return jnp.clip(jax.random.normal(key, (PACKED_TOKENS, KEY_VALUE_HEADS * HEAD_SIZE), jnp.float32), -6.0, 6.0).astype(jnp.bfloat16)


def steps_of(key, dims, split, low, high):
    factor_of = 1.0
    for position, parts in split:
        steps = jax.random.uniform(jax.random.fold_in(jax.random.fold_in(key, 6), position), (parts,), jnp.float32, low / len(split), high / len(split))
        factor_of = factor_of * jnp.repeat(jnp.exp(steps), dims[position] // parts).reshape((-1,) + (1,) * (len(dims) - 1 - position))
    return factor_of


def profile(count, total, reach, skew):
    loads = [(1 << 20) // math.isqrt(standing ** skew) + 1 for standing in range(2, count + 1)]
    spare, holding = total - reach - (count - 1), [1] * (count - 1)
    while spare > 0:
        free = [i for i in range(count - 1) if holding[i] < reach]
        mass, remaining = sum([loads[i] for i in free]), spare
        for i in free:
            more = min(reach - holding[i], max(1, remaining * loads[i] // mass), spare)
            holding[i] = holding[i] + more
            spare = spare - more
    return np.array([reach] + holding)


def uneven_parts(rng, number_of, total, limit, lean):
    if number_of == 2:
        one = jax.random.randint(rng, (), max(1, total - limit), min(limit, total - 1) + 1)
        return jnp.stack([one, total - one])
    lengths = jnp.asarray(profile(number_of, total, limit, lean), jnp.int32)
    pairs = (number_of - 1) // 2
    giver, receiver = lengths[1:1 + 2 * pairs:2], lengths[2:2 + 2 * pairs:2]
    room = jnp.minimum(giver - 1, limit - receiver)
    shifted = jax.random.randint(jax.random.fold_in(rng, 1), (pairs,), 0, 1 << 20) % (room + 1)
    lengths = lengths.at[1:1 + 2 * pairs:2].set(giver - shifted).at[2:2 + 2 * pairs:2].set(receiver + shifted)
    return lengths[jax.random.permutation(jax.random.fold_in(rng, 2), number_of)]


def gaussian(rng, dims, spread, most, split=(), kind=jnp.bfloat16):
    factor_of = steps_of(rng, dims, split, -0.22, 0.18) if split else 1.0
    drawn = jax.random.normal(rng, dims, jnp.float32) * spread * factor_of
    return jnp.minimum(jnp.maximum(drawn, -most), most).astype(kind)


def setup_inputs(seed: int = 0) -> dict:
    key_list = jax.random.split(jax.random.key(seed), 7)
    queries = draw_queries(jax.random.fold_in(key_list[6], 71), 0)
    keys = draw_keys(jax.random.fold_in(key_list[6], 71), 0)
    values = gaussian(key_list[2], (PACKED_TOKENS, KEY_VALUE_HEADS * HEAD_SIZE), 1.0, 6.0, ((0, 32), (1, 4)))
    out_weight = gaussian(key_list[3], (D, QUERY_HEAD_COUNT * HEAD_SIZE), (QUERY_HEAD_COUNT * HEAD_SIZE) ** -0.5, 0.09375, ((1, 4),))
    out_grad = gaussian(key_list[4], (PACKED_TOKENS, D), 1.0, 6.0, ((0, 32), (1, 4)))
    doc_lengths = uneven_parts(key_list[5], NDOCS, PACKED_TOKENS, MAXDOC, 2).astype(jnp.int32)
    return dict(queries=queries, keys=keys, values=values, out_weight=out_weight, out_grad=out_grad, doc_lengths=doc_lengths)


def document_of(doc_lengths, positions):
    doc_ends = jnp.cumsum(doc_lengths).astype(jnp.int32)
    return jnp.sum((positions[:, None] >= doc_ends[None, :]).astype(jnp.int32), axis=1).astype(jnp.int32)


def probabilities(query_heads, key_heads, query_pos, key_pos, doc_lengths):
    scores = jnp.einsum("igkd,jgd->gkij", query_heads, key_heads) * (HEAD_SIZE ** -0.5)
    same_doc = document_of(doc_lengths, query_pos)[:, None] == document_of(doc_lengths, key_pos)[None, :]
    allowed = same_doc & (key_pos[None, :] <= query_pos[:, None]) & (key_pos[None, :] >= 0)
    masked = jnp.where(allowed, scores, -1e30)
    row_max = jnp.max(masked, axis=-1, keepdims=True)
    row_sum = jnp.sum(jnp.exp(masked - row_max), axis=-1, keepdims=True)
    return jnp.exp(masked - (row_max + jnp.log(row_sum)))


def reference(queries, keys, values, out_weight, out_grad, doc_lengths):
    tok_rows = TOK_DEV
    key_span = (REACH + 1) * tok_rows
    groups = keys.shape[1] // HEAD_SIZE
    per_group = queries.shape[1] // HEAD_SIZE // groups
    zero_pad = jnp.zeros((REACH * tok_rows, keys.shape[1]), keys.dtype)
    keys_pad = jnp.concatenate([zero_pad, keys], axis=0)
    values_pad = jnp.concatenate([zero_pad, values], axis=0)
    block_ids = jnp.arange(PACKED_TOKENS // tok_rows, dtype=jnp.int32)

    def window(block_index):
        start = (block_index * tok_rows).astype(jnp.int32)
        query_heads = lax.dynamic_slice_in_dim(queries, start, tok_rows, 0).astype(jnp.float32).reshape(tok_rows, groups, per_group, HEAD_SIZE)
        key_heads = lax.dynamic_slice_in_dim(keys_pad, start, key_span, 0).astype(jnp.float32).reshape(key_span, groups, HEAD_SIZE)
        value_heads = lax.dynamic_slice_in_dim(values_pad, start, key_span, 0).astype(jnp.float32).reshape(key_span, groups, HEAD_SIZE)
        query_pos = start + jnp.arange(tok_rows, dtype=jnp.int32)
        key_pos = start - REACH * tok_rows + jnp.arange(key_span, dtype=jnp.int32)
        exact_probs = probabilities(query_heads, key_heads, query_pos, key_pos, doc_lengths)
        return start, query_heads, key_heads, value_heads, exact_probs

    def forward(carried, block_index):
        start, query_heads, key_heads, value_heads, exact_probs = window(block_index)
        rounded_probs = exact_probs.astype(jnp.bfloat16).astype(jnp.float32)
        block_out = jnp.einsum("gkij,jgd->igkd", rounded_probs, value_heads).reshape(tok_rows, -1)
        return carried, block_out.astype(jnp.bfloat16)

    unused, attn_blocks = lax.scan(forward, jnp.zeros((), jnp.float32), block_ids)
    attention = attn_blocks.reshape(PACKED_TOKENS, -1)
    layer_out = lax.dot_general(attention, out_weight, (((1,), (1,)), ((), ())), preferred_element_type=jnp.float32).astype(jnp.bfloat16)
    attn_grad = jnp.dot(out_grad, out_weight, preferred_element_type=jnp.float32).astype(jnp.bfloat16)
    weight_grad = lax.dot_general(out_grad, attention, (((0,), (0,)), ((), ())), preferred_element_type=jnp.float32).astype(jnp.bfloat16)

    def backward(carried, block_index):
        key_acc, value_acc = carried
        start, query_heads, key_heads, value_heads, exact_probs = window(block_index)
        rounded_probs = exact_probs.astype(jnp.bfloat16).astype(jnp.float32)
        grad_heads = lax.dynamic_slice_in_dim(attn_grad, start, tok_rows, 0).astype(jnp.float32).reshape(tok_rows, groups, per_group, HEAD_SIZE)
        attn_heads = lax.dynamic_slice_in_dim(attention, start, tok_rows, 0).astype(jnp.float32).reshape(tok_rows, groups, per_group, HEAD_SIZE)
        row_dots = jnp.einsum("igkd,igkd->gki", grad_heads, attn_heads)
        prob_grads = jnp.einsum("igkd,jgd->gkij", grad_heads, value_heads)
        score_grads = (exact_probs * (prob_grads - row_dots[..., None]) * (HEAD_SIZE ** -0.5)).astype(jnp.bfloat16).astype(jnp.float32)
        block_qgrad = jnp.einsum("gkij,jgd->igkd", score_grads, key_heads).reshape(tok_rows, -1).astype(jnp.bfloat16)
        key_terms = jnp.einsum("gkij,igkd->jgd", score_grads, query_heads).reshape(key_span, -1)
        value_terms = jnp.einsum("gkij,igkd->jgd", rounded_probs, grad_heads).reshape(key_span, -1)
        key_acc = lax.dynamic_update_slice_in_dim(key_acc, lax.dynamic_slice_in_dim(key_acc, start, key_span, 0) + key_terms, start, 0)
        value_acc = lax.dynamic_update_slice_in_dim(value_acc, lax.dynamic_slice_in_dim(value_acc, start, key_span, 0) + value_terms, start, 0)
        return (key_acc, value_acc), block_qgrad

    zero_acc = jnp.zeros(keys_pad.shape, jnp.float32)
    (key_acc, value_acc), qgrad_blocks = lax.scan(backward, (zero_acc, zero_acc), block_ids)
    query_grad = qgrad_blocks.reshape(PACKED_TOKENS, -1)
    key_grad = key_acc[REACH * tok_rows:].astype(jnp.bfloat16)
    value_grad = value_acc[REACH * tok_rows:].astype(jnp.bfloat16)
    return layer_out, query_grad, key_grad, value_grad, weight_grad
```

```python
import math

import jax
import jax.numpy as jnp
from jax import lax
from jax.experimental import pallas as pl
from jax.experimental.pallas import tpu as pltpu
from jax.sharding import PartitionSpec as P

BF = jnp.bfloat16
F32 = jnp.float32
HD = 128
TOK = 256
SIDE = 4
SCALE = HD**-0.5
EXP2_SCALE = SCALE * math.log2(math.e)
MASKED = -1e30
VMEM_LIMIT = 48 * 1024 * 1024
VM = pltpu.VMEM
SM = pltpu.SMEM


def dot_nn(a, b):
    return lax.dot_general(a, b, (((1,), (0,)), ((), ())), preferred_element_type=F32)


def dot_nt(a, b):
    return lax.dot_general(a, b, (((1,), (1,)), ((), ())), preferred_element_type=F32)


def seq_route(step):
    pairs = []
    for x in range(SIDE):
        for y in range(SIDE):
            for core in range(2):
                to = step(x, y, core)
                if to is not None:
                    pairs.append(((x * SIDE + y) * 2 + core, (to[0] * SIDE + to[1]) * 2 + to[2]))
    return pairs


def chip_step(x, y, core, chips, to_core):
    chip = x * SIDE + y + chips
    return (chip // SIDE, chip % SIDE, to_core) if 0 <= chip < SIDE * SIDE else None


SWAP = seq_route(lambda x, y, c: (x, y, 1 - c))
NEXT_CHIP = seq_route(lambda x, y, c: chip_step(x, y, c, 1, c))
MIXED = seq_route(lambda x, y, c: (x, y, 1) if c == 0 else chip_step(x, y, c, 2, 0))


def back(route):
    return [(b, a) for a, b in route]


def along(axis, d):
    if axis == "x":
        return seq_route(lambda x, y, c: ((x + d) % SIDE, y, c))
    return seq_route(lambda x, y, c: (x, (y + d) % SIDE, c))


def seq_send(v, route):
    return lax.ppermute(v, "seq", route)


def kv_send(v, d):
    return lax.ppermute(v, "kv", [(i, (i + d) % SIDE) for i in range(SIDE)])


def call(kernel, out_shape, n_in, scratch=(), smem_in=0, flops=0, transcendentals=0, moved=0):
    return pl.pallas_call(
        kernel,
        out_shape=out_shape,
        in_specs=[pl.BlockSpec(memory_space=SM)] * smem_in + [pl.BlockSpec(memory_space=VM)] * n_in,
        out_specs=jax.tree.map(lambda _: pl.BlockSpec(memory_space=VM), out_shape),
        scratch_shapes=list(scratch),
        compiler_params=pltpu.CompilerParams(vmem_limit_bytes=VMEM_LIMIT),
        cost_estimate=pl.CostEstimate(
            flops=flops, transcendentals=transcendentals, bytes_accessed=moved
        ),
    )


def split_kernel(info, g, k, v, mine, theirs, kv):
    core = info[0] % 2
    for y in range(SIDE):
        there = pl.ds(y * HD, HD)
        mine[:, there] = g[:, pl.ds(pl.multiple_of(y * 2 * HD + core * HD, HD), HD)]
        theirs[:, there] = g[:, pl.ds(pl.multiple_of(y * 2 * HD + (1 - core) * HD, HD), HD)]
    kv[:, : 2 * HD] = k[...]
    kv[:, 2 * HD :] = v[...]


def doc_starts(lengths, pos):
    def step(n, carry):
        end, start = carry
        end = end + lengths[n]
        return end, jnp.where(pos >= end, end, start)

    return lax.fori_loop(0, 64, step, (jnp.int32(0), jnp.zeros_like(pos)))[1]


def window(info, lengths, blocks):
    seq = info[0]
    core = seq % 2
    first = seq * TOK
    pos = first + lax.broadcasted_iota(jnp.int32, (1, TOK), 1)
    start = doc_starts(lengths, pos)
    own, chip_before, mixed, swapped = blocks
    mixed_at = jnp.where(core == 1, -1, -3)
    swapped_at = jnp.where(core == 1, -3, -1)
    out = []
    for ref, at in ((own, 0), (chip_before, -2), (mixed, mixed_at), (swapped, swapped_at)):
        key_pos = first + at * TOK + lax.broadcasted_iota(jnp.int32, (TOK, 1), 0)
        ok = (key_pos >= start) & (key_pos <= pos)
        out.append((ref, jnp.where(ok, 0.0, MASKED).astype(F32)))
    return out


def heads(ref, g):
    return jnp.concatenate([ref[:, pl.ds((4 * g + h) * HD, HD)] for h in range(4)], axis=0)


def fwd_kernel(info, lengths, q, own, chip_before, mixed, swapped, att, lse, scores, bias):
    for b, (_, mask) in enumerate(window(info, lengths, (own, chip_before, mixed, swapped))):
        bias[b] = mask
    refs = (own, chip_before, mixed, swapped)
    for g in range(2):
        qg = heads(q, g)
        top = jnp.full((1, 4 * TOK), MASKED, F32)
        for b, ref in enumerate(refs):
            s = dot_nt(ref[:, pl.ds(g * HD, HD)], qg) * EXP2_SCALE
            s = s + jnp.concatenate([bias[b]] * 4, axis=1)
            scores[b] = s
            top = jnp.maximum(top, jnp.max(s, axis=0, keepdims=True))
        total = jnp.zeros((1, 4 * TOK), F32)
        o = jnp.zeros((HD, 4 * TOK), F32)
        for b, ref in enumerate(refs):
            e = jnp.exp2(scores[b] - top)
            total = total + jnp.sum(e, axis=0, keepdims=True)
            o = o + dot_nn(ref[:, pl.ds((2 + g) * HD, HD)].T, e.astype(BF))
        lse[g : g + 1, :] = top + jnp.log2(total)
        o = (o / total).T
        for h in range(4):
            att[:, pl.ds((4 * g + h) * HD, HD)] = o[h * TOK : (h + 1) * TOK].astype(BF)


def bwd_kernel(
    info, lengths, q, own, chip_before, mixed, swapped, lse, att, grad_own, grad_other,
    dq, d_own, d_chip_before, d_mixed, d_swapped, bias, grad,
):
    for b, (_, mask) in enumerate(window(info, lengths, (own, chip_before, mixed, swapped))):
        bias[b] = mask
    grad[...] = (grad_own[...] + grad_other[...].astype(F32)).astype(BF)
    refs = (own, chip_before, mixed, swapped)
    outs = (d_own, d_chip_before, d_mixed, d_swapped)
    for g in range(2):
        qg = heads(q, g)
        og = heads(grad, g)
        ag = heads(att, g)
        dots = jnp.sum((og.astype(F32) * ag.astype(F32)).T, axis=0, keepdims=True)
        row_lse = lse[g : g + 1, :]
        dqt = jnp.zeros((HD, 4 * TOK), F32)
        for b, (ref, out) in enumerate(zip(refs, outs)):
            kb = ref[:, pl.ds(g * HD, HD)]
            vb = ref[:, pl.ds((2 + g) * HD, HD)]
            s = dot_nt(kb, qg) * EXP2_SCALE + jnp.concatenate([bias[b]] * 4, axis=1)
            p = jnp.exp2(s - row_lse)
            out[:, pl.ds((2 + g) * HD, HD)] = dot_nn(p.astype(BF), og).astype(out.dtype)
            ds = (p * (dot_nt(vb, og) - dots) * SCALE).astype(BF)
            out[:, pl.ds(g * HD, HD)] = dot_nn(ds, qg).astype(out.dtype)
            dqt = dqt + dot_nn(kb.T, ds)
        dqs = dqt.T
        for h in range(4):
            dq[:, pl.ds((4 * g + h) * HD, HD)] = dqs[h * TOK : (h + 1) * TOK].astype(BF)


def out_kernel(att, w, out):
    out[...] = dot_nt(att[...], w[...]).astype(BF)


def layer_out_terms(att, w):
    rows = 512
    return pl.pallas_call(
        out_kernel,
        grid=(w.shape[0] // rows,),
        in_specs=[
            pl.BlockSpec(att.shape, lambda i: (0, 0)),
            pl.BlockSpec((rows, w.shape[1]), lambda i: (i, 0)),
        ],
        out_specs=pl.BlockSpec((TOK, rows), lambda i: (0, i)),
        out_shape=jax.ShapeDtypeStruct((TOK, w.shape[0]), BF),
        compiler_params=pltpu.CompilerParams(vmem_limit_bytes=VMEM_LIMIT),
        cost_estimate=pl.CostEstimate(
            flops=2 * TOK * w.size, transcendentals=0, bytes_accessed=2 * w.size
        ),
    )(att, w)


def attn_grad_kernel(info, g0, gm, gp, g2a, g2b, w, own, other, total):
    j = pl.program_id(0)
    wb = w[...].reshape(4 * HD, w.shape[-1])

    @pl.when(j == 0)
    def _():
        total[...] = dot_nn(g0[...], wb)

    @pl.when(j == 1)
    def _():
        total[...] += dot_nn(gm[...], wb)

    @pl.when(j == 2)
    def _():
        total[...] += dot_nn(gp[...], wb)

    @pl.when(j == 3)
    def _():
        own[...] = total[:TOK] + dot_nn(g2a[...], wb)
        other[...] = (total[TOK:] + dot_nn(g2b[...], wb)).astype(BF)


def attn_grad_terms(info, parts, w):
    cols = w.shape[1]
    def w_at(j, info):
        rel = jnp.where(j == 1, 1, jnp.where(j == 2, 3, jnp.where(j == 3, 2, 0)))
        return ((info[1] + rel) % SIDE, info[0] % 2, 0, 0)

    whole = [pl.BlockSpec(p.shape, lambda j, info: (0, 0)) for p in parts]
    return pl.pallas_call(
        attn_grad_kernel,
        grid_spec=pltpu.PrefetchScalarGridSpec(
            num_scalar_prefetch=1,
            grid=(SIDE,),
            in_specs=whole + [pl.BlockSpec((SIDE, 1, HD, cols), w_at)],
            out_specs=[pl.BlockSpec((TOK, cols), lambda j, info: (0, 0))] * 2,
            scratch_shapes=[VM((2 * TOK, cols), F32)],
        ),
        out_shape=[
            jax.ShapeDtypeStruct((TOK, cols), F32),
            jax.ShapeDtypeStruct((TOK, cols), BF),
        ],
        compiler_params=pltpu.CompilerParams(vmem_limit_bytes=VMEM_LIMIT),
        cost_estimate=pl.CostEstimate(
            flops=2 * TOK * w.size, transcendentals=0, bytes_accessed=w.size
        ),
    )(info, *parts, w.reshape(SIDE * SIDE, 2, HD, cols))


def weight_kernel(info, g0, gm, gp, g2a, g2b, att, att_other, *rest):
    by_x, by_y, gt, a = rest[:4], rest[4:8], rest[8], rest[9]
    seq, z = info[0], info[1]
    y = (seq // 2) % SIDE
    x = seq // (2 * SIDE)
    a[:TOK] = att[...]
    a[TOK:] = att_other[...]
    gt[z] = g0[...].T
    gt[(z + 1) % SIDE] = gm[...].T
    gt[(z + 3) % SIDE] = gp[...].T
    gt[(z + 2) % SIDE, :, :TOK] = g2a[...].T
    gt[(z + 2) % SIDE, :, TOK:] = g2b[...].T
    half = a.shape[1] // 2
    for d in (1, 3, 2, 0):
        by_x[d][...] = dot_nn(gt[(x + d) % SIDE], a[:, :half]).astype(BF)
        rows = pl.ds(pl.multiple_of(((y + d) % SIDE) * HD, HD), HD)
        for k in range(SIDE):
            by_y[d][pl.ds(k * HD, HD), :] = dot_nn(gt[k, rows, :], a[:, half:]).astype(BF)


def weight_sum_kernel(info, *refs):
    from_x, from_y, to_y, to_x = refs[:4], refs[4:8], refs[8:12], refs[12:16]
    seq = info[0]
    y = (seq // 2) % SIDE
    x = seq // (2 * SIDE)
    for sources, outs, at in ((from_x, to_y, y), (from_y, to_x, x)):
        for d in (1, 3, 2, 0):
            rows = pl.ds(pl.multiple_of(((at + d) % SIDE) * HD, HD), HD)
            total = sources[0][rows, :].astype(F32)
            for s in sources[1:]:
                total = total + s[rows, :].astype(F32)
            outs[d][...] = total.astype(BF)


def sum_last_kernel(*refs):
    out = refs[8]
    half = out.shape[1] // 2
    for i in range(2):
        total = refs[4 * i][...].astype(F32)
        for s in refs[4 * i + 1 : 4 * i + 4]:
            total = total + s[...].astype(F32)
        out[:, i * half : (i + 1) * half] = total.astype(BF)


def weight_gradient(info, parts, att, att_other):
    cols = att.shape[1]
    half = cols // 2
    terms = call(
        weight_kernel,
        [jax.ShapeDtypeStruct((4 * HD, half), BF)] * 8,
        len(parts) + 2,
        scratch=[VM((SIDE, 4 * HD, 2 * TOK), BF), VM((2 * TOK, cols), BF)],
        smem_in=1,
        flops=2 * 2048 * 512 * cols,
        moved=7 * 2**20,
    )(info, *parts, att, att_other)
    by_x, by_y = terms[:4], terms[4:]
    from_x, from_y = [by_x[0], None, None, None], [by_y[0], None, None, None]
    for d in (1, 3, 2):
        from_x[d] = seq_send(by_x[d], along("x", d))
        from_y[d] = seq_send(by_y[d], along("y", d))
    sums = call(
        weight_sum_kernel,
        [jax.ShapeDtypeStruct((HD, half), BF)] * 8,
        8,
        smem_in=1,
        flops=4 * 2**20,
        moved=5 * 2**20,
    )(info, *from_x, *from_y)
    to_y, to_x = sums[:4], sums[4:]
    last_x, last_y = [to_x[0]], [to_y[0]]
    for d in (1, 3, 2):
        last_y.append(seq_send(to_y[d], along("y", d)))
        last_x.append(seq_send(to_x[d], along("x", d)))
    return call(
        sum_last_kernel, jax.ShapeDtypeStruct((HD, cols), BF), 8, flops=2**20, moved=5 * 2**18
    )(*last_y, *last_x)


def finish_kernel(own, chip_before, mixed, dk, dv):
    total = own[...] + chip_before[...].astype(F32) + mixed[...].astype(F32)
    dk[...] = total[:, : 2 * HD].astype(BF)
    dv[...] = total[:, 2 * HD :].astype(BF)


def per_device(queries, keys, values, out_weight, out_grad, doc_lengths):
    shape = jax.ShapeDtypeStruct
    info = jnp.stack([lax.axis_index("seq"), lax.axis_index("kv")]).astype(jnp.int32)
    cols = queries.shape[1]
    mine, theirs, kv = call(
        split_kernel, [shape((TOK, 4 * HD), BF)] * 3, 3, smem_in=1, moved=2 * 2**20
    )(info, out_grad, keys, values)

    chip_before = seq_send(kv, NEXT_CHIP)
    other_half = seq_send(theirs, SWAP)
    mixed = seq_send(kv, MIXED)
    swapped = seq_send(chip_before, SWAP)

    g0 = jnp.concatenate([mine, other_half], axis=0)
    gp = kv_send(g0, 1)
    gm = kv_send(g0, -1)
    g2a = kv_send(gp[:TOK], 1)
    g2b = kv_send(gm[TOK:], -1)
    parts = (g0, gm, gp, g2a, g2b)

    tile = 2 * TOK * 4 * TOK
    att, lse = call(
        fwd_kernel,
        [shape((TOK, cols), BF), shape((2, 4 * TOK), F32)],
        5,
        scratch=[VM((4, TOK, 4 * TOK), F32), VM((4, TOK, TOK), F32)],
        smem_in=2,
        flops=8 * tile * HD * 2,
        transcendentals=8 * tile,
        moved=2 * 2**20,
    )(info, doc_lengths, queries, kv, chip_before, mixed, swapped)

    att_other = seq_send(att, SWAP)
    layer_out = lax.psum_scatter(
        layer_out_terms(att, out_weight), "kv", scatter_dimension=1, tiled=True
    )

    weight_grad = weight_gradient(info, parts, att, att_other)

    grad_own, grad_to_other = attn_grad_terms(info, parts, out_weight)
    grad_other = seq_send(grad_to_other, SWAP)
    query_grad, d_own, d_chip_before, d_mixed, d_swapped = call(
        bwd_kernel,
        [
            shape((TOK, cols), BF),
            shape((TOK, 4 * HD), F32),
            shape((TOK, 4 * HD), F32),
            shape((TOK, 4 * HD), BF),
            shape((TOK, 4 * HD), BF),
        ],
        9,
        scratch=[VM((4, TOK, TOK), F32), VM((TOK, cols), BF)],
        smem_in=2,
        flops=8 * tile * HD * 5,
        transcendentals=8 * tile,
        moved=6 * 2**20,
    )(info, doc_lengths, queries, kv, chip_before, mixed, swapped, lse, att, grad_own, grad_other)
    from_mixed = seq_send(d_mixed, back(MIXED))
    from_swapped = seq_send(d_swapped, SWAP)
    from_chip = seq_send(
        (d_chip_before + from_swapped.astype(F32)).astype(BF), back(NEXT_CHIP)
    )
    key_grad, value_grad = call(
        finish_kernel, [shape((TOK, 2 * HD), BF)] * 2, 3, flops=2**20, moved=2**20
    )(d_own, from_chip, from_mixed)
    return (layer_out, query_grad, key_grad, value_grad, weight_grad)


def solution(mesh):
    placed = (P("seq", "kv"), P("seq", "kv"), P("seq", "kv"), P(None, "kv"), P("seq", "kv"), P())
    return jax.shard_map(
        per_device,
        mesh=mesh,
        in_specs=placed,
        out_specs=(P("seq", "kv"),) * 5,
        check_vma=False,
    )
```

```python
import math

import jax
import jax.numpy as jnp
from jax import lax
from jax.experimental import pallas as pl
from jax.experimental.pallas import tpu as pltpu
from jax.sharding import PartitionSpec as P

BF = jnp.bfloat16
F32 = jnp.float32
HD = 128
TOK = 256
SIDE = 4
SCALE = HD**-0.5
EXP2_SCALE = SCALE * math.log2(math.e)
MASKED = -1e30
VMEM_LIMIT = 24 * 1024 * 1024
VM = pltpu.VMEM
SM = pltpu.SMEM


def dot_nn(a, b):
    return lax.dot_general(a, b, (((1,), (0,)), ((), ())), preferred_element_type=F32)


def dot_nt(a, b):
    return lax.dot_general(a, b, (((1,), (1,)), ((), ())), preferred_element_type=F32)


def seq_route(step):
    pairs = []
    for x in range(SIDE):
        for y in range(SIDE):
            for core in range(2):
                to = step(x, y, core)
                if to is not None:
                    pairs.append(((x * SIDE + y) * 2 + core, (to[0] * SIDE + to[1]) * 2 + to[2]))
    return pairs


def chip_step(x, y, core, chips, to_core):
    chip = x * SIDE + y + chips
    return (chip // SIDE, chip % SIDE, to_core) if 0 <= chip < SIDE * SIDE else None


SWAP = seq_route(lambda x, y, c: (x, y, 1 - c))
NEXT_CHIP = seq_route(lambda x, y, c: chip_step(x, y, c, 1, c))
MIXED = seq_route(lambda x, y, c: (x, y, 1) if c == 0 else chip_step(x, y, c, 2, 0))


def back(route):
    return [(b, a) for a, b in route]


def toward(core):
    return 1 - 2 * core


def along(axis, step):
    if axis == "x":
        return seq_route(lambda x, y, c: ((x + step(c)) % SIDE, y, c))
    return seq_route(lambda x, y, c: (x, (y + step(c)) % SIDE, c))


def same(core):
    return toward(core)


def opposite(core):
    return -toward(core)


def across(core):
    return 2


def seq_send(v, route):
    return lax.ppermute(v, "seq", route)


def kv_send(v, step):
    pairs = []
    for seq in range(2 * SIDE * SIDE):
        for z in range(SIDE):
            pairs.append((seq * SIDE + z, seq * SIDE + (z + step(seq % 2)) % SIDE))
    return lax.ppermute(v, ("seq", "kv"), pairs)


def call(kernel, out_shape, n_in, scratch=(), smem_in=0, flops=1000, transcendentals=0, moved=1000):
    return pl.pallas_call(
        kernel,
        out_shape=out_shape,
        in_specs=[pl.BlockSpec(memory_space=SM)] * smem_in + [pl.BlockSpec(memory_space=VM)] * n_in,
        out_specs=jax.tree.map(lambda _: pl.BlockSpec(memory_space=VM), out_shape),
        scratch_shapes=list(scratch),
        compiler_params=pltpu.CompilerParams(vmem_limit_bytes=VMEM_LIMIT),
        cost_estimate=pl.CostEstimate(
            flops=flops, transcendentals=transcendentals, bytes_accessed=moved
        ),
    )


def doc_starts(lengths, pos):
    def step(n, carry):
        end, start = carry
        end = end + lengths[n]
        return end, jnp.where(pos >= end, end, start)

    return lax.fori_loop(0, 64, step, (jnp.int32(0), jnp.zeros_like(pos)))[1]


def window(info, lengths, blocks):
    seq = info[0]
    core = seq % 2
    first = seq * TOK
    pos = first + lax.broadcasted_iota(jnp.int32, (1, TOK), 1)
    start = doc_starts(lengths, pos)
    own, chip_before, mixed, swapped = blocks
    mixed_at = jnp.where(core == 1, -1, -3)
    swapped_at = jnp.where(core == 1, -3, -1)
    out = []
    for ref, at in ((own, 0), (chip_before, -2), (mixed, mixed_at), (swapped, swapped_at)):
        key_pos = first + at * TOK + lax.broadcasted_iota(jnp.int32, (TOK, 1), 0)
        ok = (key_pos >= start) & (key_pos <= pos)
        out.append((ref, jnp.where(ok, 0.0, MASKED).astype(F32)))
    return out


def heads(ref, g):
    return jnp.concatenate([ref[:, pl.ds((4 * g + h) * HD, HD)] for h in range(4)], axis=0)


def fwd_kernel(info, lengths, q, own, chip_before, mixed, swapped, att, lse, scores, bias):
    for b, (_, mask) in enumerate(window(info, lengths, (own, chip_before, mixed, swapped))):
        bias[b] = mask
    refs = (own, chip_before, mixed, swapped)
    for g in range(2):
        qg = heads(q, g)
        top = jnp.full((1, 4 * TOK), MASKED, F32)
        for b, ref in enumerate(refs):
            s = dot_nt(ref[:, pl.ds(g * HD, HD)], qg) * EXP2_SCALE
            s = s + jnp.concatenate([bias[b]] * 4, axis=1)
            scores[b] = s
            top = jnp.maximum(top, jnp.max(s, axis=0, keepdims=True))
        total = jnp.zeros((1, 4 * TOK), F32)
        o = jnp.zeros((HD, 4 * TOK), F32)
        for b, ref in enumerate(refs):
            e = jnp.exp2(scores[b] - top)
            total = total + jnp.sum(e, axis=0, keepdims=True)
            o = o + dot_nn(ref[:, pl.ds((2 + g) * HD, HD)].T, e.astype(BF))
        lse[g : g + 1, :] = top + jnp.log2(total)
        o = (o / total).T
        for h in range(4):
            att[:, pl.ds((4 * g + h) * HD, HD)] = o[h * TOK : (h + 1) * TOK].astype(BF)


def bwd_kernel(
    info, lengths, q, own, chip_before, mixed, swapped, lse, att, attn_grad,
    dq, d_own, d_chip_before, d_mixed, d_swapped, bias,
):
    for b, (_, mask) in enumerate(window(info, lengths, (own, chip_before, mixed, swapped))):
        bias[b] = mask
    refs = (own, chip_before, mixed, swapped)
    outs = (d_own, d_chip_before, d_mixed, d_swapped)
    for g in range(2):
        qg = heads(q, g)
        og = heads(attn_grad, g)
        ag = heads(att, g)
        dots = jnp.sum((og.astype(F32) * ag.astype(F32)).T, axis=0, keepdims=True)
        row_lse = lse[g : g + 1, :]
        dqt = jnp.zeros((HD, 4 * TOK), F32)
        for b, (ref, out) in enumerate(zip(refs, outs)):
            kb = ref[:, pl.ds(g * HD, HD)]
            vb = ref[:, pl.ds((2 + g) * HD, HD)]
            s = dot_nt(kb, qg) * EXP2_SCALE + jnp.concatenate([bias[b]] * 4, axis=1)
            p = jnp.exp2(s - row_lse)
            out[:, pl.ds((2 + g) * HD, HD)] = dot_nn(p.astype(BF), og).astype(out.dtype)
            ds = (p * (dot_nt(vb, og) - dots) * SCALE).astype(BF)
            out[:, pl.ds(g * HD, HD)] = dot_nn(ds, qg).astype(out.dtype)
            dqt = dqt + dot_nn(kb.T, ds)
        dqs = dqt.T
        for h in range(4):
            dq[:, pl.ds((4 * g + h) * HD, HD)] = dqs[h * TOK : (h + 1) * TOK].astype(BF)


def finish_kernel(own, chip_before, mixed, dk, dv):
    total = own[...] + chip_before[...].astype(F32) + mixed[...].astype(F32)
    dk[...] = total[:, : 2 * HD].astype(BF)
    dv[...] = total[:, 2 * HD :].astype(BF)


def chunk(ref, at, size):
    return ref[pl.ds(pl.multiple_of((at % SIDE) * size, size), size), :]


def out_first_kernel(info, att, w, across_out, opposite_out):
    z, way = info[1], 1 - 2 * (info[0] % 2)
    rows = w.shape[0] // SIDE
    across_out[...] = dot_nt(att[...], chunk(w, z + 2, rows)).astype(BF)
    opposite_out[...] = dot_nt(att[...], chunk(w, z + SIDE - way, rows)).astype(BF)


def out_second_kernel(info, att, w, relayed, same_out, own):
    z, way = info[1], 1 - 2 * (info[0] % 2)
    rows = w.shape[0] // SIDE
    same = dot_nt(att[...], chunk(w, z + SIDE + way, rows)) + relayed[...].astype(F32)
    same_out[...] = same.astype(BF)
    own[...] = dot_nt(att[...], chunk(w, z, rows))


def attn_grad_kernel(info, g, first, second, third, w, out):
    z, way = info[1], 1 - 2 * (info[0] % 2)
    rows = w.shape[0] // SIDE
    total = dot_nn(g[...], chunk(w, z, rows))
    total = total + dot_nn(first[...], chunk(w, z + SIDE - way, rows))
    total = total + dot_nn(second[...], chunk(w, z + SIDE + way, rows))
    total = total + dot_nn(third[...], chunk(w, z + 2, rows))
    out[...] = total.astype(BF)


def place(info):
    seq = info[0]
    core = seq % 2
    return seq // (2 * SIDE), (seq // 2) % SIDE, info[1], core, 1 - 2 * core


def weight_terms(gt, a, k, by_x):
    half = a.shape[1] // 2
    if by_x:
        return dot_nn(gt[k % SIDE], a[:, :half])
    rows = pl.ds(pl.multiple_of((k % SIDE) * HD, HD), HD)
    lhs = jnp.concatenate([gt[x, rows, :] for x in range(SIDE)], axis=0)
    return dot_nn(lhs, a[:, half:])


def weight_across_kernel(info, *refs):
    here, there, att, att_there, gt, a, x_out, y_out = refs[:4], refs[4:8], *refs[8:]
    x, y, z, core, way = place(info)
    a[:TOK] = att[...]
    a[TOK:] = att_there[...]
    for t, sources, w in ((0, here, way), (1, there, -way)):
        for source, at in zip(sources, (z, z + SIDE - w, z + SIDE + w, z + 2)):
            for k in range(SIDE):
                columns = pl.ds(pl.multiple_of(k * 2 * HD + core * HD, HD), HD)
                gt[at % SIDE, k * HD : (k + 1) * HD, t * TOK : (t + 1) * TOK] = source[:, columns].T
    x_out[...] = weight_terms(gt, a, x + 2, True).astype(BF)
    y_out[...] = weight_terms(gt, a, y + 2, False).astype(BF)


def weight_opposite_kernel(info, gt, a, x_out, y_out):
    x, y, z, core, way = place(info)
    x_out[...] = weight_terms(gt, a, x + SIDE - way, True).astype(BF)
    y_out[...] = weight_terms(gt, a, y + SIDE - way, False).astype(BF)


def weight_same_kernel(info, gt, a, x_relayed, y_relayed, x_out, y_out, x_own, y_own):
    x, y, z, core, way = place(info)
    x_same = weight_terms(gt, a, x + SIDE + way, True) + x_relayed[...].astype(F32)
    x_out[...] = x_same.astype(BF)
    y_same = weight_terms(gt, a, y + SIDE + way, False) + y_relayed[...].astype(F32)
    y_out[...] = y_same.astype(BF)
    x_own[...] = weight_terms(gt, a, x, True)
    y_own[...] = weight_terms(gt, a, y, False)


def weight_sum_kernel(info, *refs):
    x, y, z, core, way = place(info)
    for sources, outs, at in ((refs[:3], refs[6:10], y), (refs[3:6], refs[10:14], x)):
        for out, to in zip(outs, (at + SIDE + way, at + SIDE - way, at + 2, at)):
            total = chunk(sources[0], to, HD)
            for s in sources[1:]:
                total = total + chunk(s, to, HD).astype(F32)
            out[...] = total.astype(out.dtype)


def sum_last_kernel(*refs):
    out = refs[8]
    half = out.shape[1] // 2
    for i in range(2):
        total = refs[4 * i][...]
        for s in refs[4 * i + 1 : 4 * i + 4]:
            total = total + s[...].astype(F32)
        out[:, i * half : (i + 1) * half] = total.astype(BF)


def weight_gradient(info, here, there, att, att_there):
    cols = att.shape[1]
    half = cols // 2
    piece = jax.ShapeDtypeStruct((4 * HD, half), BF)
    piece32 = jax.ShapeDtypeStruct((4 * HD, half), F32)
    gt, a, x_across, y_across = call(
        weight_across_kernel,
        [
            jax.ShapeDtypeStruct((SIDE, 4 * HD, 2 * TOK), BF),
            jax.ShapeDtypeStruct((2 * TOK, cols), BF),
            piece,
            piece,
        ],
        10,
        smem_in=1,
    )(info, *here, *there, att, att_there)
    x_relayed = seq_send(x_across, along("x", same))
    y_relayed = seq_send(y_across, along("y", same))
    x_opp, y_opp = call(weight_opposite_kernel, [piece] * 2, 2, smem_in=1)(info, gt, a)
    x_from_opp = seq_send(x_opp, along("x", opposite))
    y_from_opp = seq_send(y_opp, along("y", opposite))
    x_same, y_same, x_own, y_own = call(
        weight_same_kernel, [piece] * 2 + [piece32] * 2, 4, smem_in=1
    )(info, gt, a, x_relayed, y_relayed)
    x_from_same = seq_send(x_same, along("x", same))
    y_from_same = seq_send(y_same, along("y", same))
    strip = jax.ShapeDtypeStruct((HD, half), BF)
    strip32 = jax.ShapeDtypeStruct((HD, half), F32)
    sums = call(weight_sum_kernel, ([strip] * 3 + [strip32]) * 2, 6, smem_in=1)(
        info, x_own, x_from_opp, x_from_same, y_own, y_from_opp, y_from_same
    )
    last = []
    for axis, terms in (("y", sums[:4]), ("x", sums[4:])):
        last.append(terms[3])
        for term, step in zip(terms, (same, opposite, across)):
            last.append(seq_send(term, along(axis, step)))
    return call(sum_last_kernel, jax.ShapeDtypeStruct((HD, cols), BF), 8)(*last)


def per_device(queries, keys, values, out_weight, out_grad, doc_lengths):
    shape = jax.ShapeDtypeStruct
    info = jnp.stack([lax.axis_index("seq"), lax.axis_index("kv")]).astype(jnp.int32)
    cols = queries.shape[1]

    first = kv_send(out_grad, same)
    second = kv_send(out_grad, opposite)
    third = kv_send(first, same)
    here = (out_grad, first, second, third)
    there = tuple(seq_send(v, SWAP) for v in here)

    kv = jnp.concatenate([keys, values], axis=1)
    chip_before = seq_send(kv, NEXT_CHIP)
    mixed = seq_send(kv, MIXED)
    swapped = seq_send(chip_before, SWAP)

    att, lse = call(
        fwd_kernel,
        [shape((TOK, cols), BF), shape((2, 4 * TOK), F32)],
        5,
        scratch=[VM((4, TOK, 4 * TOK), F32), VM((4, TOK, TOK), F32)],
        smem_in=2,
    )(info, doc_lengths, queries, kv, chip_before, mixed, swapped)
    att_there = seq_send(att, SWAP)

    block = shape((TOK, cols), BF)
    out_across, out_opp = call(out_first_kernel, [block] * 2, 2, smem_in=1)(info, att, out_weight)
    out_relayed = kv_send(out_across, same)
    out_from_opp = kv_send(out_opp, opposite)
    out_same, out_own = call(out_second_kernel, [block, shape((TOK, cols), F32)], 3, smem_in=1)(
        info, att, out_weight, out_relayed
    )
    out_from_same = kv_send(out_same, same)
    layer_out = (out_own + out_from_opp.astype(F32) + out_from_same.astype(F32)).astype(BF)

    weight_grad = weight_gradient(info, here, there, att, att_there)

    attn_grad = call(attn_grad_kernel, block, 5, smem_in=1)(info, *here, out_weight)
    query_grad, d_own, d_chip_before, d_mixed, d_swapped = call(
        bwd_kernel,
        [
            block,
            shape((TOK, 4 * HD), F32),
            shape((TOK, 4 * HD), F32),
            shape((TOK, 4 * HD), BF),
            shape((TOK, 4 * HD), BF),
        ],
        8,
        scratch=[VM((4, TOK, TOK), F32)],
        smem_in=2,
    )(info, doc_lengths, queries, kv, chip_before, mixed, swapped, lse, att, attn_grad)
    from_mixed = seq_send(d_mixed, back(MIXED))
    from_swapped = seq_send(d_swapped, SWAP)
    from_chip = seq_send((d_chip_before + from_swapped.astype(F32)).astype(BF), back(NEXT_CHIP))
    key_grad, value_grad = call(finish_kernel, [shape((TOK, 2 * HD), BF)] * 2, 3)(
        d_own, from_chip, from_mixed
    )
    return (layer_out, query_grad, key_grad, value_grad, weight_grad)


def solution(mesh):
    placed = (P("seq", "kv"), P("seq", "kv"), P("seq", "kv"), P(None, "kv"), P("seq", "kv"), P())
    return jax.shard_map(
        per_device,
        mesh=mesh,
        in_specs=placed,
        out_specs=(P("seq", "kv"),) * 5,
        check_vma=False,
    )
```

```python
import math

import jax
import jax.numpy as jnp
from jax import lax
from jax.experimental import pallas as pl
from jax.experimental.pallas import tpu as pltpu
from jax.sharding import PartitionSpec as P

BF = jnp.bfloat16
F32 = jnp.float32
HD = 128
TOK = 256
SIDE = 4
SCALE = HD**-0.5
EXP2_SCALE = SCALE * math.log2(math.e)
MASKED = -1e30
HBM_BYTES_PER_US = 50_000
VM = pltpu.VMEM
SM = pltpu.SMEM


def dot_nn(a, b):
    return lax.dot_general(a, b, (((1,), (0,)), ((), ())), preferred_element_type=F32)


def dot_nt(a, b):
    return lax.dot_general(a, b, (((1,), (1,)), ((), ())), preferred_element_type=F32)


def seq_route(step):
    pairs = []
    for x in range(SIDE):
        for y in range(SIDE):
            for core in range(2):
                to = step(x, y, core)
                if to is not None:
                    pairs.append(((x * SIDE + y) * 2 + core, (to[0] * SIDE + to[1]) * 2 + to[2]))
    return pairs


def chips_on(x, y, chips, core):
    chip = (x * SIDE + y + chips) % (SIDE * SIDE)
    return (chip // SIDE, chip % SIDE, core)


SWAP = seq_route(lambda x, y, c: (x, y, 1 - c))
NEXT_CHIP = seq_route(lambda x, y, c: chips_on(x, y, 1, c))
MIXED = seq_route(lambda x, y, c: (x, y, 1) if c == 0 else chips_on(x, y, 2, 0))


def back(route):
    return [(b, a) for a, b in route]


def by_core(axis_of_core, step):
    def to(x, y, c):
        if axis_of_core[c] == "x":
            return ((x + step) % SIDE, y, c)
        return (x, (y + step) % SIDE, c)

    return seq_route(to)


def same(core):
    return 1 - 2 * core


def opposite(core):
    return 2 * core - 1


def seq_send(v, route):
    return lax.ppermute(v, "seq", route)


def kv_send(v, step):
    pairs = []
    for seq in range(2 * SIDE * SIDE):
        for z in range(SIDE):
            pairs.append((seq * SIDE + z, seq * SIDE + (z + step(seq % 2)) % SIDE))
    return lax.ppermute(v, ("seq", "kv"), pairs)


def call(
    kernel, out_shape, n_in, us, scratch=(), smem_in=0, hbm_in=0, after=0, vmem_mib=24
):
    def body(*refs):
        n = smem_in + hbm_in + n_in
        kernel(*refs[:n], *refs[n + after :])

    vmem = pl.BlockSpec(memory_space=VM)
    return pl.pallas_call(
        body,
        out_shape=out_shape,
        in_specs=[pl.BlockSpec(memory_space=SM)] * smem_in
        + [pl.BlockSpec(memory_space=pltpu.HBM)] * hbm_in
        + [vmem] * n_in
        + [pl.BlockSpec(memory_space=pl.ANY)] * after,
        out_specs=jax.tree.map(lambda _: vmem, out_shape),
        scratch_shapes=list(scratch),
        compiler_params=pltpu.CompilerParams(vmem_limit_bytes=vmem_mib * 2**20),
        cost_estimate=pl.CostEstimate(
            flops=0, transcendentals=0, bytes_accessed=int(us * HBM_BYTES_PER_US)
        ),
    )


def doc_starts(lengths, pos):
    def step(n, carry):
        end, start = carry
        end = end + lengths[n]
        return end, jnp.where(pos >= end, end, start)

    return lax.fori_loop(0, 64, step, (jnp.int32(0), jnp.zeros_like(pos)))[1]


def prepare_kernel(info, lengths, q, q_heads, bias):
    core = info[0] % 2
    first = info[0] * TOK
    pos = first + lax.broadcasted_iota(jnp.int32, (1, TOK), 1)
    start = doc_starts(lengths, pos)
    for b, at in enumerate((0, -2, 2 * core - 3, -1 - 2 * core)):
        key_pos = first + at * TOK + lax.broadcasted_iota(jnp.int32, (TOK, 1), 0)
        ok = (key_pos >= start) & (key_pos <= pos)
        bias[b] = jnp.where(ok, 0.0, MASKED).astype(F32)
    for g in range(2):
        q_heads[g] = heads(q, g)


def heads(ref, g):
    return jnp.concatenate([ref[:, pl.ds((4 * g + h) * HD, HD)] for h in range(4)], axis=0)


def fwd_kernel(q, bias, own, two, mixed, swapped, att, lse, scores):
    refs = (own, two, mixed, swapped)
    for g in range(2):
        qg = q[g]
        top = jnp.full((1, 4 * TOK), MASKED, F32)
        for b, ref in enumerate(refs):
            s = dot_nt(ref[:, pl.ds(g * HD, HD)], qg) * EXP2_SCALE
            s = s + jnp.concatenate([bias[b]] * 4, axis=1)
            scores[b] = s
            top = jnp.maximum(top, jnp.max(s, axis=0, keepdims=True))
        total = jnp.zeros((1, 4 * TOK), F32)
        o = jnp.zeros((HD, 4 * TOK), F32)
        for b, ref in enumerate(refs):
            e = jnp.exp2(scores[b] - top)
            total = total + jnp.sum(e, axis=0, keepdims=True)
            o = o + dot_nn(ref[:, pl.ds((2 + g) * HD, HD)].T, e.astype(BF))
        lse[g : g + 1, :] = top + jnp.log2(total)
        o = (o / total).T
        for h in range(4):
            att[:, pl.ds((4 * g + h) * HD, HD)] = o[h * TOK : (h + 1) * TOK].astype(BF)


def bwd_kernel(
    q, bias, own, two, mixed, swapped, lse, att, attn_grad, dq, d_own, d_two, d_mixed, d_swapped
):
    refs = (own, two, mixed, swapped)
    outs = (d_own, d_two, d_mixed, d_swapped)
    for g in range(2):
        qg = q[g]
        og = heads(attn_grad, g)
        ag = heads(att, g)
        dots = jnp.sum((og.astype(F32) * ag.astype(F32)).T, axis=0, keepdims=True)
        row_lse = lse[g : g + 1, :]
        dqt = jnp.zeros((HD, 4 * TOK), F32)
        for b, (ref, out) in enumerate(zip(refs, outs)):
            kb = ref[:, pl.ds(g * HD, HD)]
            vb = ref[:, pl.ds((2 + g) * HD, HD)]
            s = dot_nt(kb, qg) * EXP2_SCALE + jnp.concatenate([bias[b]] * 4, axis=1)
            p = jnp.exp2(s - row_lse)
            out[:, pl.ds((2 + g) * HD, HD)] = dot_nn(p.astype(BF), og).astype(out.dtype)
            ds = (p * (dot_nt(vb, og) - dots) * SCALE).astype(BF)
            out[:, pl.ds(g * HD, HD)] = dot_nn(ds, qg).astype(out.dtype)
            dqt = dqt + dot_nn(kb.T, ds)
        dqs = dqt.T
        for h in range(4):
            dq[:, pl.ds((4 * g + h) * HD, HD)] = dqs[h * TOK : (h + 1) * TOK].astype(BF)


def finish_kernel(own, from_mixed, from_two, dk, dv):
    total = own[...] + from_mixed[...].astype(F32) + from_two[...].astype(F32)
    dk[...] = total[:, : 2 * HD].astype(BF)
    dv[...] = total[:, 2 * HD :].astype(BF)


def layer_sum_kernel(own, from_opp, from_same, out):
    total = own[...] + from_opp[...].astype(F32) + from_same[...].astype(F32)
    out[...] = total.astype(BF)


def stream(info, w, w_here, sems, order):
    rows = w_here.shape[1]
    copies = []
    for i, at in enumerate(order):
        source = w.at[pl.ds(pl.multiple_of((at % SIDE) * rows, rows), rows), :]
        copies.append(pltpu.make_async_copy(source, w_here.at[i], sems.at[i]))
        copies[-1].start()
    for i, copy in enumerate(copies):
        copy.wait()
        yield i, w_here[i]


def out_kernel(info, w, att, across, opp, same_term, own, w_here, sems):
    z, way = info[1], 1 - 2 * (info[0] % 2)
    outs = (across, opp, same_term, own)
    order = (z + 2, z + SIDE - way, z + SIDE + way, z)
    for i, rows in stream(info, w, w_here, sems, order):
        outs[i][...] = dot_nt(att[...], rows).astype(outs[i].dtype)


def add_kernel(a, b, out):
    out[...] = (a[...] + b[...].astype(F32)).astype(BF)


def attn_grad_kernel(info, w, g, first, second, third, out, w_here, sems):
    z, way = info[1], 1 - 2 * (info[0] % 2)
    parts = (g, first, second, third)
    order = (z, z + SIDE - way, z + SIDE + way, z + 2)
    total = None
    for i, rows in stream(info, w, w_here, sems, order):
        term = dot_nn(parts[i][...], rows)
        total = term if total is None else total + term
    out[...] = total.astype(BF)


def place(info):
    seq = info[0]
    core = seq % 2
    x, y = seq // (2 * SIDE), (seq // 2) % SIDE
    return core, jnp.where(core == 0, x, y), jnp.where(core == 0, y, x)


def weight_kernel(info, *refs):
    here, there, att, att_there, across, plus, minus, own, g, a = refs[:4], refs[4:8], *refs[8:]
    core, at, _ = place(info)
    z, way = info[1], 1 - 2 * core
    half = a.shape[1]
    columns = pl.ds(pl.multiple_of(core * half, half), half)
    a[:TOK] = att[:, columns]
    a[TOK:] = att_there[:, columns]
    for t, sources, w in ((0, here, way), (1, there, -way)):
        for source, chunk_at in zip(sources, (z, z + SIDE - w, z + SIDE + w, z + 2)):
            g[chunk_at % SIDE, t * TOK : (t + 1) * TOK, :] = source[...]
    outs = ((across, 2), (plus, 1), (minus, SIDE - 1), (own, 0))

    @pl.when(core == 0)
    def _():
        for out, step in outs:
            out[...] = dot_nn(g[(at + step) % SIDE].T, a[...]).astype(out.dtype)

    @pl.when(core == 1)
    def _():
        for out, step in outs:
            strip = pl.ds(pl.multiple_of(((at + step) % SIDE) * TOK, TOK), TOK)
            for x in range(SIDE):
                terms = dot_nn(g[x, :, strip].T, a[...])
                out[x * TOK : (x + 1) * TOK, :] = terms.astype(out.dtype)


def weight_sum_kernel(info, own, from_minus, from_plus, from_across, plus, minus, across, mine):
    core, _, at = place(info)
    for out, step in ((plus, 1), (minus, SIDE - 1), (across, 2), (mine, 0)):
        rows = pl.ds(pl.multiple_of(((at + step) % SIDE) * TOK, TOK), TOK)
        total = own[rows, :] + from_minus[rows, :].astype(F32) + from_plus[rows, :].astype(F32)
        out[...] = (total + from_across[rows, :].astype(F32)).astype(out.dtype)


def weight_halves_kernel(info, mine, a, b, c, keep, give):
    core = info[0] % 2
    for out, rows_of in ((keep, core), (give, 1 - core)):
        rows = pl.ds(pl.multiple_of(rows_of * HD, HD), HD)
        total = mine[rows, :] + a[rows, :].astype(F32) + b[rows, :].astype(F32)
        out[...] = (total + c[rows, :].astype(F32)).astype(BF)


def weight_join_kernel(info, kept, given, out):
    half = kept.shape[1]
    core = info[0] % 2
    out[:, pl.ds(pl.multiple_of(core * half, half), half)] = kept[...]
    out[:, pl.ds(pl.multiple_of((1 - core) * half, half), half)] = given[...]


def per_device(queries, keys, values, out_weight, out_grad, doc_lengths):
    shape = jax.ShapeDtypeStruct
    info = jnp.stack([lax.axis_index("seq"), lax.axis_index("kv")]).astype(jnp.int32)
    cols = queries.shape[1]
    half = cols // 2
    block = shape((TOK, cols), BF)

    first = kv_send(out_grad, same)
    second = kv_send(out_grad, opposite)

    own = jnp.pad(keys, ((0, 0), (0, 2 * HD))) + jnp.pad(values, ((0, 0), (2 * HD, 0)))
    two = seq_send(own, NEXT_CHIP)
    mixed = seq_send(own, MIXED)
    q, bias = call(
        prepare_kernel,
        [shape((2, 4 * TOK, HD), BF), shape((4, TOK, TOK), F32)],
        1,
        us=4,
        smem_in=2,
    )(info, doc_lengths, queries)
    q, bias, mixed, two, first, second = lax.optimization_barrier(
        (q, bias, mixed, two, first, second)
    )
    swapped = seq_send(two, SWAP)
    third = kv_send(first, same)
    here = (out_grad, first, second, third)
    there = tuple(seq_send(v, SWAP) for v in here)
    blocks = (own, two, mixed, swapped)

    att, lse = call(
        fwd_kernel,
        [block, shape((2, 4 * TOK), F32)],
        6,
        us=4,
        scratch=[VM((4, TOK, 4 * TOK), F32)],
    )(q, bias, *blocks)
    att_there = seq_send(att, SWAP)

    chunks = [VM((SIDE, cols, cols), BF), pltpu.SemaphoreType.DMA((SIDE,))]
    block32 = shape((TOK, cols), F32)
    out_across, out_opp, out_same, out_own = call(
        out_kernel,
        [block] * 2 + [block32] * 2,
        1,
        us=4,
        smem_in=1,
        hbm_in=1,
        after=3,
        scratch=chunks,
        vmem_mib=48,
    )(info, out_weight, att, *there[:3])
    pieces = shape((4 * TOK, half), BF)
    across, plus, minus, weight_own = call(
        weight_kernel,
        [pieces] * 3 + [shape((4 * TOK, half), F32)],
        10,
        us=4,
        smem_in=1,
        after=1,
        scratch=[VM((SIDE, 2 * TOK, 4 * TOK), BF), VM((2 * TOK, half), BF)],
    )(info, *here, *there, att, att_there, out_across)
    stage = ("x", "y")
    from_across = seq_send(across, by_core(stage, 2))
    from_minus = seq_send(plus, by_core(stage, 1))
    from_plus = seq_send(minus, by_core(stage, -1))

    attn_grad = call(
        attn_grad_kernel, block, 4, us=4, smem_in=1, hbm_in=1, after=1, scratch=chunks, vmem_mib=48
    )(info, out_weight, *here, plus)
    out_relayed = kv_send(out_across, same)
    out_from_opp = kv_send(out_opp, opposite)

    out_same = call(add_kernel, block, 2, us=1, after=1)(out_same, out_relayed, attn_grad)
    out_from_same = kv_send(out_same, same)
    part = shape((TOK, 4 * HD), F32)
    part16 = shape((TOK, 4 * HD), BF)
    query_grad, d_own, d_two, d_mixed, d_swapped = call(
        bwd_kernel, [block, part, part, part16, part16], 9, us=6.5, after=1
    )(q, bias, *blocks, lse, att, attn_grad, out_same)
    layer_out = call(layer_sum_kernel, block, 3, us=1, after=1)(
        out_own, out_from_opp, out_from_same, d_own
    )
    from_swapped = seq_send(d_swapped, SWAP)
    from_mixed = seq_send(d_mixed, back(MIXED))
    d_two = call(add_kernel, part16, 2, us=1, after=1)(d_two, from_swapped, layer_out)
    from_two = seq_send(d_two, back(NEXT_CHIP))

    strip = shape((TOK, half), BF)
    plus, minus, across, mine = call(
        weight_sum_kernel,
        [strip] * 3 + [shape((TOK, half), F32)],
        4,
        us=1,
        smem_in=1,
        after=1,
    )(info, weight_own, from_minus, from_plus, from_across, d_two)
    stage = ("y", "x")
    last = [
        seq_send(across, by_core(stage, 2)),
        seq_send(plus, by_core(stage, 1)),
        seq_send(minus, by_core(stage, -1)),
    ]
    kept, given = call(weight_halves_kernel, [shape((HD, half), BF)] * 2, 4, us=1, smem_in=1)(
        info, mine, *last
    )
    key_grad, value_grad = call(finish_kernel, [shape((TOK, 2 * HD), BF)] * 2, 3, us=1, after=1)(
        d_own, from_mixed, from_two, given
    )
    weight_grad = call(weight_join_kernel, shape((HD, cols), BF), 2, us=1, smem_in=1, after=1)(
        info, kept, seq_send(given, SWAP), key_grad
    )
    return (layer_out, query_grad, key_grad, value_grad, weight_grad)


def solution(mesh):
    placed = (P("seq", "kv"), P("seq", "kv"), P("seq", "kv"), P(None, "kv"), P("seq", "kv"), P())
    return jax.shard_map(
        per_device,
        mesh=mesh,
        in_specs=placed,
        out_specs=(P("seq", "kv"),) * 5,
        check_vma=False,
    )
```

```python
import math

import jax
import jax.numpy as jnp
from jax import lax
from jax.experimental import pallas as pl
from jax.experimental.pallas import tpu as pltpu
from jax.sharding import PartitionSpec as P

BF = jnp.bfloat16
F32 = jnp.float32
HD = 128
TOK = 256
SIDE = 4
SCALE = HD**-0.5
EXP2_SCALE = SCALE * math.log2(math.e)
MASKED = -1e30
HBM_BYTES_PER_US = 50_000
VM = pltpu.VMEM
SM = pltpu.SMEM


def dot_nn(a, b):
    return lax.dot_general(a, b, (((1,), (0,)), ((), ())), preferred_element_type=F32)


def dot_nt(a, b):
    return lax.dot_general(a, b, (((1,), (1,)), ((), ())), preferred_element_type=F32)


def seq_route(step):
    pairs = []
    for x in range(SIDE):
        for y in range(SIDE):
            for core in range(2):
                to = step(x, y, core)
                if to is not None:
                    pairs.append(((x * SIDE + y) * 2 + core, (to[0] * SIDE + to[1]) * 2 + to[2]))
    return pairs


def chips_on(x, y, chips, core):
    chip = (x * SIDE + y + chips) % (SIDE * SIDE)
    return (chip // SIDE, chip % SIDE, core)


SWAP = seq_route(lambda x, y, c: (x, y, 1 - c))
NEXT_CHIP = seq_route(lambda x, y, c: chips_on(x, y, 1, c))
MIXED = seq_route(lambda x, y, c: (x, y, 1) if c == 0 else chips_on(x, y, 2, 0))


def back(route):
    return [(b, a) for a, b in route]


def by_core(axis_of_core, step):
    def to(x, y, c):
        if axis_of_core[c] == "x":
            return ((x + step) % SIDE, y, c)
        return (x, (y + step) % SIDE, c)

    return seq_route(to)


def same(core):
    return 1 - 2 * core


def opposite(core):
    return 2 * core - 1


def seq_send(v, route):
    return lax.ppermute(v, "seq", route)


def kv_send(v, step):
    pairs = []
    for seq in range(2 * SIDE * SIDE):
        for z in range(SIDE):
            pairs.append((seq * SIDE + z, seq * SIDE + (z + step(seq % 2)) % SIDE))
    return lax.ppermute(v, ("seq", "kv"), pairs)


def call(
    kernel, out_shape, n_in, us, scratch=(), smem_in=0, hbm_in=0, after=0, vmem_mib=24
):
    def body(*refs):
        n = smem_in + hbm_in + n_in
        kernel(*refs[:n], *refs[n + after :])

    vmem = pl.BlockSpec(memory_space=VM)
    return pl.pallas_call(
        body,
        out_shape=out_shape,
        in_specs=[pl.BlockSpec(memory_space=SM)] * smem_in
        + [pl.BlockSpec(memory_space=pltpu.HBM)] * hbm_in
        + [vmem] * n_in
        + [pl.BlockSpec(memory_space=pl.ANY)] * after,
        out_specs=jax.tree.map(lambda _: vmem, out_shape),
        scratch_shapes=list(scratch),
        compiler_params=pltpu.CompilerParams(vmem_limit_bytes=vmem_mib * 2**20),
        cost_estimate=pl.CostEstimate(
            flops=0, transcendentals=0, bytes_accessed=int(us * HBM_BYTES_PER_US)
        ),
    )


def doc_starts(lengths, pos):
    def step(n, carry):
        end, start = carry
        end = end + lengths[n]
        return end, jnp.where(pos >= end, end, start)

    return lax.fori_loop(0, 64, step, (jnp.int32(0), jnp.zeros_like(pos)))[1]


def prepare_kernel(info, lengths, q, q_heads, bias):
    core = info[0] % 2
    first = info[0] * TOK
    pos = first + lax.broadcasted_iota(jnp.int32, (1, TOK), 1)
    start = doc_starts(lengths, pos)
    for b, at in enumerate((0, -2, 2 * core - 3, -1 - 2 * core)):
        key_pos = first + at * TOK + lax.broadcasted_iota(jnp.int32, (TOK, 1), 0)
        ok = (key_pos >= start) & (key_pos <= pos)
        bias[b] = jnp.where(ok, 0.0, MASKED).astype(F32)
    for g in range(2):
        q_heads[g] = heads(q, g)


def heads(ref, g):
    return jnp.concatenate([ref[:, pl.ds((4 * g + h) * HD, HD)] for h in range(4)], axis=0)


def fwd_kernel(q, bias, own, two, mixed, swapped, att, lse, scores):
    refs = (own, two, mixed, swapped)
    for g in range(2):
        qg = q[g]
        top = jnp.full((1, 4 * TOK), MASKED, F32)
        for b, ref in enumerate(refs):
            s = dot_nt(ref[:, pl.ds(g * HD, HD)], qg) * EXP2_SCALE
            s = s + jnp.concatenate([bias[b]] * 4, axis=1)
            scores[b] = s
            top = jnp.maximum(top, jnp.max(s, axis=0, keepdims=True))
        total = jnp.zeros((1, 4 * TOK), F32)
        o = jnp.zeros((HD, 4 * TOK), F32)
        for b, ref in enumerate(refs):
            e = jnp.exp2(scores[b] - top)
            total = total + jnp.sum(e, axis=0, keepdims=True)
            o = o + dot_nn(ref[:, pl.ds((2 + g) * HD, HD)].T, e.astype(BF))
        lse[g : g + 1, :] = top + jnp.log2(total)
        o = (o / total).T
        for h in range(4):
            att[:, pl.ds((4 * g + h) * HD, HD)] = o[h * TOK : (h + 1) * TOK].astype(BF)


def bwd_kernel(
    q, bias, own, two, mixed, swapped, lse, att, attn_grad, dq, d_own, d_two, d_mixed, d_swapped
):
    refs = (own, two, mixed, swapped)
    outs = (d_own, d_two, d_mixed, d_swapped)
    for g in range(2):
        qg = q[g]
        og = heads(attn_grad, g)
        ag = heads(att, g)
        dots = jnp.sum((og.astype(F32) * ag.astype(F32)).T, axis=0, keepdims=True)
        row_lse = lse[g : g + 1, :]
        dqt = jnp.zeros((HD, 4 * TOK), F32)
        for b, (ref, out) in enumerate(zip(refs, outs)):
            kb = ref[:, pl.ds(g * HD, HD)]
            vb = ref[:, pl.ds((2 + g) * HD, HD)]
            s = dot_nt(kb, qg) * EXP2_SCALE + jnp.concatenate([bias[b]] * 4, axis=1)
            p = jnp.exp2(s - row_lse)
            out[:, pl.ds((2 + g) * HD, HD)] = dot_nn(p.astype(BF), og).astype(out.dtype)
            ds = (p * (dot_nt(vb, og) - dots) * SCALE).astype(BF)
            out[:, pl.ds(g * HD, HD)] = dot_nn(ds, qg).astype(out.dtype)
            dqt = dqt + dot_nn(kb.T, ds)
        dqs = dqt.T
        for h in range(4):
            dq[:, pl.ds((4 * g + h) * HD, HD)] = dqs[h * TOK : (h + 1) * TOK].astype(BF)


def finish_kernel(own, from_mixed, from_two, dk, dv, token):
    total = own[...] + from_mixed[...].astype(F32) + from_two[...].astype(F32)
    dk[...] = total[:, : 2 * HD].astype(BF)
    dv[...] = total[:, 2 * HD :].astype(BF)
    token[...] = jnp.zeros_like(token)


def layer_sum_kernel(own, from_opp, from_same, out, token):
    total = own[...] + from_opp[...].astype(F32) + from_same[...].astype(F32)
    out[...] = total.astype(BF)
    token[...] = jnp.zeros_like(token)


def chunk(ref, at, size):
    return ref[pl.ds(pl.multiple_of((at % SIDE) * size, size), size), :]


def out_first_kernel(info, att, w, across, opp):
    z, way = info[1], 1 - 2 * (info[0] % 2)
    rows = w.shape[0] // SIDE
    across[...] = dot_nt(att[...], chunk(w, z + 2, rows)).astype(BF)
    opp[...] = dot_nt(att[...], chunk(w, z + SIDE - way, rows)).astype(BF)


def out_second_kernel(info, att, w, relayed, same_out, own):
    z, way = info[1], 1 - 2 * (info[0] % 2)
    rows = w.shape[0] // SIDE
    term = dot_nt(att[...], chunk(w, z + SIDE + way, rows))
    same_out[...] = (term + relayed[...].astype(F32)).astype(BF)
    own[...] = dot_nt(att[...], chunk(w, z, rows))


def add_kernel(a, b, out):
    out[...] = (a[...] + b[...].astype(F32)).astype(BF)


def attn_grad_kernel(info, g, first, second, third, w, out):
    z, way = info[1], 1 - 2 * (info[0] % 2)
    rows = w.shape[0] // SIDE
    total = dot_nn(g[...], chunk(w, z, rows))
    total = total + dot_nn(first[...], chunk(w, z + SIDE - way, rows))
    total = total + dot_nn(second[...], chunk(w, z + SIDE + way, rows))
    total = total + dot_nn(third[...], chunk(w, z + 2, rows))
    out[...] = total.astype(BF)


def place(info):
    seq = info[0]
    core = seq % 2
    x, y = seq // (2 * SIDE), (seq // 2) % SIDE
    return core, jnp.where(core == 0, x, y), jnp.where(core == 0, y, x)


def weight_terms(info, g, a, outs):
    core, at, _ = place(info)

    @pl.when(core == 0)
    def _():
        for out, step in outs:
            out[...] = dot_nn(g[(at + step) % SIDE].T, a[...]).astype(out.dtype)

    @pl.when(core == 1)
    def _():
        for out, step in outs:
            strip = pl.ds(pl.multiple_of(((at + step) % SIDE) * TOK, TOK), TOK)
            for x in range(SIDE):
                terms = dot_nn(g[x, :, strip].T, a[...])
                out[x * TOK : (x + 1) * TOK, :] = terms.astype(out.dtype)


def weight_across_kernel(info, *refs):
    here, there, att, att_there, across, g, a = refs[:4], refs[4:8], *refs[8:]
    core, z = info[0] % 2, info[1]
    way = 1 - 2 * core
    half = a.shape[1]
    columns = pl.ds(pl.multiple_of(core * half, half), half)
    a[:TOK] = att[:, columns]
    a[TOK:] = att_there[:, columns]
    for t, sources, w in ((0, here, way), (1, there, -way)):
        for source, chunk_at in zip(sources, (z, z + SIDE - w, z + SIDE + w, z + 2)):
            g[chunk_at % SIDE, t * TOK : (t + 1) * TOK, :] = source[...]
    weight_terms(info, g, a, ((across, 2),))


def weight_next_kernel(info, g, a, plus, minus, own):
    weight_terms(info, g, a, ((plus, 1), (minus, SIDE - 1), (own, 0)))


def weight_sum_kernel(info, own, from_minus, from_plus, from_across, plus, minus, across, mine):
    core, _, at = place(info)
    for out, step in ((plus, 1), (minus, SIDE - 1), (across, 2), (mine, 0)):
        rows = pl.ds(pl.multiple_of(((at + step) % SIDE) * TOK, TOK), TOK)
        total = own[rows, :] + from_minus[rows, :].astype(F32) + from_plus[rows, :].astype(F32)
        out[...] = (total + from_across[rows, :].astype(F32)).astype(out.dtype)


def weight_halves_kernel(info, mine, a, b, c, keep, give):
    core = info[0] % 2
    for out, rows_of in ((keep, core), (give, 1 - core)):
        rows = pl.ds(pl.multiple_of(rows_of * HD, HD), HD)
        total = mine[rows, :] + a[rows, :].astype(F32) + b[rows, :].astype(F32)
        out[...] = (total + c[rows, :].astype(F32)).astype(BF)


def weight_join_kernel(info, kept, given, out):
    half = kept.shape[1]
    core = info[0] % 2
    out[:, pl.ds(pl.multiple_of(core * half, half), half)] = kept[...]
    out[:, pl.ds(pl.multiple_of((1 - core) * half, half), half)] = given[...]


def per_device(queries, keys, values, out_weight, out_grad, doc_lengths):
    shape = jax.ShapeDtypeStruct
    info = jnp.stack([lax.axis_index("seq"), lax.axis_index("kv")]).astype(jnp.int32)
    cols = queries.shape[1]
    half = cols // 2
    block = shape((TOK, cols), BF)

    own = jnp.pad(keys, ((0, 0), (0, 2 * HD))) + jnp.pad(values, ((0, 0), (2 * HD, 0)))
    two = seq_send(own, NEXT_CHIP)
    mixed = seq_send(own, MIXED)

    first = kv_send(out_grad, same)
    second = kv_send(lax.optimization_barrier((out_grad, own))[0], opposite)

    q, bias = call(
        prepare_kernel,
        [shape((2, 4 * TOK, HD), BF), shape((4, TOK, TOK), F32)],
        1,
        us=4,
        smem_in=2,
    )(info, doc_lengths, queries)
    q, bias, mixed, two, first = lax.optimization_barrier((q, bias, mixed, two, first))
    swapped = seq_send(two, SWAP)
    blocks = (own, two, mixed, swapped)

    att, lse = call(
        fwd_kernel,
        [block, shape((2, 4 * TOK), F32)],
        6,
        us=4,
        scratch=[VM((4, TOK, 4 * TOK), F32)],
    )(q, bias, *blocks)
    third = kv_send(first, same)
    first, second, _ = lax.optimization_barrier((first, second, att))
    att_there = seq_send(att, SWAP)

    out_across, out_opp = call(out_first_kernel, [block] * 2, 2, us=2, smem_in=1)(info, att, out_weight)
    out_relayed = kv_send(out_across, same)
    out_from_opp = kv_send(out_opp, opposite)

    here = (out_grad, first, second, third)
    later = lax.optimization_barrier((third, out_across))[0]
    there = tuple(seq_send(v, SWAP) for v in (out_grad, first, second, later))
    pieces = shape((4 * TOK, half), BF)
    across, g, a = call(
        weight_across_kernel,
        [pieces, shape((SIDE, 2 * TOK, 4 * TOK), BF), shape((2 * TOK, half), BF)],
        10,
        us=4,
        smem_in=1,
        after=1,
    )(info, *here, *there, att, att_there, out_across)
    stage = ("x", "y")
    from_across = seq_send(across, by_core(stage, 2))
    plus, minus, weight_own = call(
        weight_next_kernel, [pieces] * 2 + [shape((4 * TOK, half), F32)], 2, us=4, smem_in=1
    )(info, g, a)
    from_minus = seq_send(plus, by_core(stage, 1))
    from_plus = seq_send(minus, by_core(stage, -1))

    attn_grad = call(attn_grad_kernel, block, 5, us=3, smem_in=1, after=1)(
        info, *here, out_weight, plus
    )

    part = shape((TOK, 4 * HD), F32)
    part16 = shape((TOK, 4 * HD), BF)
    query_grad, d_own, d_two, d_mixed, d_swapped = call(
        bwd_kernel, [block, part, part, part16, part16], 9, us=6.5, after=2
    )(q, bias, *blocks, lse, att, attn_grad, out_relayed, out_from_opp)
    from_swapped = seq_send(d_swapped, SWAP)
    from_mixed = seq_send(d_mixed, back(MIXED))
    out_same, out_own = call(
        out_second_kernel, [block, shape((TOK, cols), F32)], 3, us=2, smem_in=1, after=1
    )(info, att, out_weight, out_relayed, d_own)
    d_two = call(add_kernel, part16, 2, us=1, after=1)(d_two, from_swapped, out_same)
    from_two = seq_send(d_two, back(NEXT_CHIP))
    out_from_same = kv_send(lax.optimization_barrier((out_same, d_two))[0], same)

    strip = shape((TOK, half), BF)
    plus, minus, across, mine = call(
        weight_sum_kernel,
        [strip] * 3 + [shape((TOK, half), F32)],
        4,
        us=1,
        smem_in=1,
        after=1,
    )(info, weight_own, from_minus, from_plus, from_across, d_two)
    stage = ("y", "x")
    last = [
        seq_send(across, by_core(stage, 2)),
        seq_send(plus, by_core(stage, 1)),
        seq_send(minus, by_core(stage, -1)),
    ]
    layer_out, token = call(layer_sum_kernel, [block, shape((8, HD), F32)], 3, us=1, after=1)(
        out_own, out_from_opp, out_from_same, across
    )
    key_grad, value_grad, token = call(
        finish_kernel, [shape((TOK, 2 * HD), BF)] * 2 + [shape((8, HD), F32)], 3, us=1, after=1
    )(d_own, from_mixed, from_two, token)
    kept, given = call(weight_halves_kernel, [shape((HD, half), BF)] * 2, 4, us=1, smem_in=1, after=1)(
        info, mine, *last, token
    )
    weight_grad = call(weight_join_kernel, shape((HD, cols), BF), 2, us=1, smem_in=1)(
        info, kept, seq_send(given, SWAP)
    )
    return (layer_out, query_grad, key_grad, value_grad, weight_grad)


def solution(mesh):
    placed = (P("seq", "kv"), P("seq", "kv"), P("seq", "kv"), P(None, "kv"), P("seq", "kv"), P())
    return jax.shard_map(
        per_device,
        mesh=mesh,
        in_specs=placed,
        out_specs=(P("seq", "kv"),) * 5,
        check_vma=False,
    )
```

```python
import math

import jax
import jax.numpy as jnp
from jax import lax
from jax.experimental import pallas as pl
from jax.experimental.pallas import tpu as pltpu
from jax.sharding import PartitionSpec as P

BF = jnp.bfloat16
F32 = jnp.float32
HD = 128
TOK = 256
SIDE = 4
SCALE = HD**-0.5
EXP2_SCALE = SCALE * math.log2(math.e)
MASKED = -1e30
HBM_BYTES_PER_US = 50_000
VM = pltpu.VMEM
SM = pltpu.SMEM


def dot_nn(a, b):
    return lax.dot_general(a, b, (((1,), (0,)), ((), ())), preferred_element_type=F32)


def dot_nt(a, b):
    return lax.dot_general(a, b, (((1,), (1,)), ((), ())), preferred_element_type=F32)


def seq_route(step):
    pairs = []
    for x in range(SIDE):
        for y in range(SIDE):
            for core in range(2):
                to = step(x, y, core)
                if to is not None:
                    pairs.append(((x * SIDE + y) * 2 + core, (to[0] * SIDE + to[1]) * 2 + to[2]))
    return pairs


def chips_on(x, y, chips, core):
    chip = (x * SIDE + y + chips) % (SIDE * SIDE)
    return (chip // SIDE, chip % SIDE, core)


SWAP = seq_route(lambda x, y, c: (x, y, 1 - c))
NEXT_CHIP = seq_route(lambda x, y, c: chips_on(x, y, 1, c))
MIXED = seq_route(lambda x, y, c: (x, y, 1) if c == 0 else chips_on(x, y, 2, 0))


def back(route):
    return [(b, a) for a, b in route]


def by_core(axis_of_core, step):
    def to(x, y, c):
        if axis_of_core[c] == "x":
            return ((x + step) % SIDE, y, c)
        return (x, (y + step) % SIDE, c)

    return seq_route(to)


def same(core):
    return 1 - 2 * core


def opposite(core):
    return 2 * core - 1


def seq_send(v, route):
    return lax.ppermute(v, "seq", route)


def kv_send(v, step):
    pairs = []
    for seq in range(2 * SIDE * SIDE):
        for z in range(SIDE):
            pairs.append((seq * SIDE + z, seq * SIDE + (z + step(seq % 2)) % SIDE))
    return lax.ppermute(v, ("seq", "kv"), pairs)


def call(
    kernel, out_shape, n_in, us, scratch=(), smem_in=0, hbm_in=0, after=0, vmem_mib=24
):
    def body(*refs):
        n = smem_in + hbm_in + n_in
        kernel(*refs[:n], *refs[n + after :])

    vmem = pl.BlockSpec(memory_space=VM)
    return pl.pallas_call(
        body,
        out_shape=out_shape,
        in_specs=[pl.BlockSpec(memory_space=SM)] * smem_in
        + [pl.BlockSpec(memory_space=pltpu.HBM)] * hbm_in
        + [vmem] * n_in
        + [pl.BlockSpec(memory_space=pl.ANY)] * after,
        out_specs=jax.tree.map(lambda _: vmem, out_shape),
        scratch_shapes=list(scratch),
        compiler_params=pltpu.CompilerParams(vmem_limit_bytes=vmem_mib * 2**20),
        cost_estimate=pl.CostEstimate(
            flops=0, transcendentals=0, bytes_accessed=int(us * HBM_BYTES_PER_US)
        ),
    )


def doc_starts(lengths, pos):
    def step(n, carry):
        end, start = carry
        end = end + lengths[n]
        return end, jnp.where(pos >= end, end, start)

    return lax.fori_loop(0, 64, step, (jnp.int32(0), jnp.zeros_like(pos)))[1]


def prepare_kernel(info, lengths, q, w, q_heads, bias):
    core = info[0] % 2
    first = info[0] * TOK
    pos = first + lax.broadcasted_iota(jnp.int32, (1, TOK), 1)
    start = doc_starts(lengths, pos)
    for b, at in enumerate((0, -2, 2 * core - 3, -1 - 2 * core)):
        key_pos = first + at * TOK + lax.broadcasted_iota(jnp.int32, (TOK, 1), 0)
        ok = (key_pos >= start) & (key_pos <= pos)
        bias[b] = jnp.where(ok, 0.0, MASKED).astype(F32)
    for g in range(2):
        q_heads[g] = heads(q, g)


def heads(ref, g):
    return jnp.concatenate([ref[:, pl.ds((4 * g + h) * HD, HD)] for h in range(4)], axis=0)


def fwd_kernel(q, bias, own, two, mixed, swapped, att, lse, scores):
    refs = (own, two, mixed, swapped)
    for g in range(2):
        qg = q[g]
        top = jnp.full((1, 4 * TOK), MASKED, F32)
        for b, ref in enumerate(refs):
            s = dot_nt(ref[:, pl.ds(g * HD, HD)], qg) * EXP2_SCALE
            s = s + jnp.concatenate([bias[b]] * 4, axis=1)
            scores[b] = s
            top = jnp.maximum(top, jnp.max(s, axis=0, keepdims=True))
        total = jnp.zeros((1, 4 * TOK), F32)
        o = jnp.zeros((HD, 4 * TOK), F32)
        for b, ref in enumerate(refs):
            e = jnp.exp2(scores[b] - top)
            total = total + jnp.sum(e, axis=0, keepdims=True)
            o = o + dot_nn(ref[:, pl.ds((2 + g) * HD, HD)].T, e.astype(BF))
        lse[g : g + 1, :] = top + jnp.log2(total)
        o = (o / total).T
        for h in range(4):
            att[:, pl.ds((4 * g + h) * HD, HD)] = o[h * TOK : (h + 1) * TOK].astype(BF)


def bwd_kernel(
    q, bias, own, two, mixed, swapped, lse, att, attn_grad, dq, d_own, d_two, d_mixed, d_swapped
):
    refs = (own, two, mixed, swapped)
    outs = (d_own, d_two, d_mixed, d_swapped)
    for g in range(2):
        qg = q[g]
        og = heads(attn_grad, g)
        ag = heads(att, g)
        dots = jnp.sum((og.astype(F32) * ag.astype(F32)).T, axis=0, keepdims=True)
        row_lse = lse[g : g + 1, :]
        dqt = jnp.zeros((HD, 4 * TOK), F32)
        for b, (ref, out) in enumerate(zip(refs, outs)):
            kb = ref[:, pl.ds(g * HD, HD)]
            vb = ref[:, pl.ds((2 + g) * HD, HD)]
            s = dot_nt(kb, qg) * EXP2_SCALE + jnp.concatenate([bias[b]] * 4, axis=1)
            p = jnp.exp2(s - row_lse)
            out[:, pl.ds((2 + g) * HD, HD)] = dot_nn(p.astype(BF), og).astype(out.dtype)
            ds = (p * (dot_nt(vb, og) - dots) * SCALE).astype(BF)
            out[:, pl.ds(g * HD, HD)] = dot_nn(ds, qg).astype(out.dtype)
            dqt = dqt + dot_nn(kb.T, ds)
        dqs = dqt.T
        for h in range(4):
            dq[:, pl.ds((4 * g + h) * HD, HD)] = dqs[h * TOK : (h + 1) * TOK].astype(BF)


def finish_kernel(own, from_mixed, from_two, dk, dv, token):
    total = own[...] + from_mixed[...].astype(F32) + from_two[...].astype(F32)
    dk[...] = total[:, : 2 * HD].astype(BF)
    dv[...] = total[:, 2 * HD :].astype(BF)
    token[...] = jnp.zeros_like(token)


def layer_sum_kernel(own, from_opp, from_same, out, token):
    total = own[...] + from_opp[...].astype(F32) + from_same[...].astype(F32)
    out[...] = total.astype(BF)
    token[...] = jnp.zeros_like(token)


def chunk(ref, at, size):
    return ref[pl.ds(pl.multiple_of((at % SIDE) * size, size), size), :]


def out_first_kernel(info, att, w, across, opp):
    z, way = info[1], 1 - 2 * (info[0] % 2)
    rows = w.shape[0] // SIDE
    across[...] = dot_nt(att[...], chunk(w, z + 2, rows)).astype(BF)
    opp[...] = dot_nt(att[...], chunk(w, z + SIDE - way, rows)).astype(BF)


def out_second_kernel(info, att, w, relayed, same_out, own):
    z, way = info[1], 1 - 2 * (info[0] % 2)
    rows = w.shape[0] // SIDE
    term = dot_nt(att[...], chunk(w, z + SIDE + way, rows))
    same_out[...] = (term + relayed[...].astype(F32)).astype(BF)
    own[...] = dot_nt(att[...], chunk(w, z, rows))


def add_kernel(a, b, out):
    out[...] = (a[...] + b[...].astype(F32)).astype(BF)


def attn_grad_kernel(info, g, first, second, third, w, out):
    z, way = info[1], 1 - 2 * (info[0] % 2)
    rows = w.shape[0] // SIDE
    total = dot_nn(g[...], chunk(w, z, rows))
    total = total + dot_nn(first[...], chunk(w, z + SIDE - way, rows))
    total = total + dot_nn(second[...], chunk(w, z + SIDE + way, rows))
    total = total + dot_nn(third[...], chunk(w, z + 2, rows))
    out[...] = total.astype(BF)


def place(info):
    seq = info[0]
    core = seq % 2
    x, y = seq // (2 * SIDE), (seq // 2) % SIDE
    return core, jnp.where(core == 0, x, y), jnp.where(core == 0, y, x)


def weight_terms(info, g, a, outs):
    core, at, _ = place(info)

    @pl.when(core == 0)
    def _():
        for out, step in outs:
            out[...] = dot_nn(g[(at + step) % SIDE].T, a[...]).astype(out.dtype)

    @pl.when(core == 1)
    def _():
        for out, step in outs:
            strip = pl.ds(pl.multiple_of(((at + step) % SIDE) * TOK, TOK), TOK)
            for x in range(SIDE):
                terms = dot_nn(g[x, :, strip].T, a[...])
                out[x * TOK : (x + 1) * TOK, :] = terms.astype(out.dtype)


def weight_across_kernel(info, *refs):
    here, there, att, att_there, across, g, a = refs[:4], refs[4:8], *refs[8:]
    core, z = info[0] % 2, info[1]
    way = 1 - 2 * core
    half = a.shape[1]
    columns = pl.ds(pl.multiple_of(core * half, half), half)
    a[:TOK] = att[:, columns]
    a[TOK:] = att_there[:, columns]
    for t, sources, w in ((0, here, way), (1, there, -way)):
        for source, chunk_at in zip(sources, (z, z + SIDE - w, z + SIDE + w, z + 2)):
            g[chunk_at % SIDE, t * TOK : (t + 1) * TOK, :] = source[...]
    weight_terms(info, g, a, ((across, 2),))


def weight_next_kernel(info, g, a, plus, minus, own):
    weight_terms(info, g, a, ((plus, 1), (minus, SIDE - 1), (own, 0)))


def weight_sum_kernel(info, own, from_minus, from_plus, from_across, plus, minus, across, mine):
    core, _, at = place(info)
    for out, step in ((plus, 1), (minus, SIDE - 1), (across, 2), (mine, 0)):
        rows = pl.ds(pl.multiple_of(((at + step) % SIDE) * TOK, TOK), TOK)
        total = own[rows, :] + from_minus[rows, :].astype(F32) + from_plus[rows, :].astype(F32)
        out[...] = (total + from_across[rows, :].astype(F32)).astype(out.dtype)


def weight_halves_kernel(info, mine, a, b, c, keep, give):
    core = info[0] % 2
    for out, rows_of in ((keep, core), (give, 1 - core)):
        rows = pl.ds(pl.multiple_of(rows_of * HD, HD), HD)
        total = mine[rows, :] + a[rows, :].astype(F32) + b[rows, :].astype(F32)
        out[...] = (total + c[rows, :].astype(F32)).astype(BF)


def weight_join_kernel(info, kept, given, out):
    half = kept.shape[1]
    core = info[0] % 2
    out[:, pl.ds(pl.multiple_of(core * half, half), half)] = kept[...]
    out[:, pl.ds(pl.multiple_of((1 - core) * half, half), half)] = given[...]


def per_device(queries, keys, values, out_weight, out_grad, doc_lengths):
    shape = jax.ShapeDtypeStruct
    info = jnp.stack([lax.axis_index("seq"), lax.axis_index("kv")]).astype(jnp.int32)
    cols = queries.shape[1]
    half = cols // 2
    block = shape((TOK, cols), BF)

    own = jnp.pad(keys, ((0, 0), (0, 2 * HD))) + jnp.pad(values, ((0, 0), (2 * HD, 0)))
    two = seq_send(own, NEXT_CHIP)
    mixed = seq_send(own, MIXED)

    first = kv_send(out_grad, same)
    second = kv_send(lax.optimization_barrier((out_grad, own))[0], opposite)

    q, bias = call(
        prepare_kernel,
        [shape((2, 4 * TOK, HD), BF), shape((4, TOK, TOK), F32)],
        2,
        us=4,
        smem_in=2,
    )(info, doc_lengths, queries, out_weight)
    q, bias, mixed, two, first = lax.optimization_barrier((q, bias, mixed, two, first))
    swapped = seq_send(two, SWAP)
    blocks = (own, two, mixed, swapped)

    att, lse = call(
        fwd_kernel,
        [block, shape((2, 4 * TOK), F32)],
        6,
        us=4,
        scratch=[VM((4, TOK, 4 * TOK), F32)],
    )(q, bias, *blocks)
    third = kv_send(first, same)
    first, second, _ = lax.optimization_barrier((first, second, att))
    att_there = seq_send(att, SWAP)

    out_across, out_opp = call(out_first_kernel, [block] * 2, 2, us=2, smem_in=1)(info, att, out_weight)

    here = (out_grad, first, second, third)
    later = lax.optimization_barrier((third, out_across))[0]
    there = tuple(seq_send(v, SWAP) for v in (out_grad, first, second, later))
    pieces = shape((4 * TOK, half), BF)
    across, g, a = call(
        weight_across_kernel,
        [pieces, shape((SIDE, 2 * TOK, 4 * TOK), BF), shape((2 * TOK, half), BF)],
        10,
        us=4,
        smem_in=1,
        after=1,
    )(info, *here, *there, att, att_there, out_across)
    stage = ("x", "y")
    from_across = seq_send(across, by_core(stage, 2))
    plus, minus, weight_own = call(
        weight_next_kernel, [pieces] * 2 + [shape((4 * TOK, half), F32)], 2, us=4, smem_in=1
    )(info, g, a)
    from_minus = seq_send(plus, by_core(stage, 1))
    from_plus = seq_send(minus, by_core(stage, -1))

    send_across, send_opp, _ = lax.optimization_barrier((out_across, out_opp, plus))
    out_relayed = kv_send(send_across, same)
    out_from_opp = kv_send(send_opp, opposite)

    attn_grad = call(attn_grad_kernel, block, 5, us=3, smem_in=1, after=1)(
        info, *here, out_weight, plus
    )

    part = shape((TOK, 4 * HD), F32)
    part16 = shape((TOK, 4 * HD), BF)
    query_grad, d_own, d_two, d_mixed, d_swapped = call(
        bwd_kernel, [block, part, part, part16, part16], 9, us=6.5
    )(q, bias, *blocks, lse, att, attn_grad)
    from_swapped = seq_send(d_swapped, SWAP)
    from_mixed = seq_send(d_mixed, back(MIXED))
    out_same, out_own = call(
        out_second_kernel, [block, shape((TOK, cols), F32)], 3, us=2, smem_in=1, after=2
    )(info, att, out_weight, out_relayed, d_own, out_from_opp)
    d_two = call(add_kernel, part16, 2, us=1, after=2)(
        d_two, from_swapped, out_same, from_across
    )
    from_two = seq_send(d_two, back(NEXT_CHIP))
    out_from_same = kv_send(lax.optimization_barrier((out_same, d_two))[0], same)

    strip = shape((TOK, half), BF)
    plus, minus, across, mine = call(
        weight_sum_kernel,
        [strip] * 3 + [shape((TOK, half), F32)],
        4,
        us=1,
        smem_in=1,
        after=1,
    )(info, weight_own, from_minus, from_plus, from_across, d_two)
    stage = ("y", "x")
    last = [
        seq_send(across, by_core(stage, 2)),
        seq_send(plus, by_core(stage, 1)),
        seq_send(minus, by_core(stage, -1)),
    ]
    layer_out, token = call(layer_sum_kernel, [block, shape((8, HD), F32)], 3, us=1, after=1)(
        out_own, out_from_opp, out_from_same, across
    )
    key_grad, value_grad, token = call(
        finish_kernel, [shape((TOK, 2 * HD), BF)] * 2 + [shape((8, HD), F32)], 3, us=1, after=2
    )(d_own, from_mixed, from_two, token, last[0])
    kept, given = call(weight_halves_kernel, [shape((HD, half), BF)] * 2, 4, us=1, smem_in=1, after=1)(
        info, mine, *last, token
    )
    weight_grad = call(weight_join_kernel, shape((HD, cols), BF), 2, us=1, smem_in=1)(
        info, kept, seq_send(given, SWAP)
    )
    return (layer_out, query_grad, key_grad, value_grad, weight_grad)


def solution(mesh):
    placed = (P("seq", "kv"), P("seq", "kv"), P("seq", "kv"), P(None, "kv"), P("seq", "kv"), P())
    return jax.shard_map(
        per_device,
        mesh=mesh,
        in_specs=placed,
        out_specs=(P("seq", "kv"),) * 5,
        check_vma=False,
    )
```

```python
import math

import jax
import jax.numpy as jnp
from jax import lax
from jax.experimental import pallas as pl
from jax.experimental.pallas import tpu as pltpu
from jax.sharding import PartitionSpec as P

BF = jnp.bfloat16
F32 = jnp.float32
HD = 128
TOK = 256
SIDE = 4
SCALE = HD**-0.5
EXP2_SCALE = SCALE * math.log2(math.e)
MASKED = -1e30
HBM_BYTES_PER_US = 50_000
VM = pltpu.VMEM
SM = pltpu.SMEM


def dot_nn(a, b):
    return lax.dot_general(a, b, (((1,), (0,)), ((), ())), preferred_element_type=F32)


def dot_nt(a, b):
    return lax.dot_general(a, b, (((1,), (1,)), ((), ())), preferred_element_type=F32)


def seq_route(step):
    pairs = []
    for x in range(SIDE):
        for y in range(SIDE):
            for core in range(2):
                to = step(x, y, core)
                if to is not None:
                    pairs.append(((x * SIDE + y) * 2 + core, (to[0] * SIDE + to[1]) * 2 + to[2]))
    return pairs


def chips_on(x, y, chips, core):
    chip = (x * SIDE + y + chips) % (SIDE * SIDE)
    return (chip // SIDE, chip % SIDE, core)


SWAP = seq_route(lambda x, y, c: (x, y, 1 - c))
NEXT_CHIP = seq_route(lambda x, y, c: chips_on(x, y, 1, c))
MIXED = seq_route(lambda x, y, c: (x, y, 1) if c == 0 else chips_on(x, y, 2, 0))


def back(route):
    return [(b, a) for a, b in route]


def by_core(axis_of_core, step):
    def to(x, y, c):
        if axis_of_core[c] == "x":
            return ((x + step) % SIDE, y, c)
        return (x, (y + step) % SIDE, c)

    return seq_route(to)


def same(core):
    return 1 - 2 * core


def opposite(core):
    return 2 * core - 1


def seq_send(v, route):
    return lax.ppermute(v, "seq", route)


def kv_send(v, step):
    pairs = []
    for seq in range(2 * SIDE * SIDE):
        for z in range(SIDE):
            pairs.append((seq * SIDE + z, seq * SIDE + (z + step(seq % 2)) % SIDE))
    return lax.ppermute(v, ("seq", "kv"), pairs)


def call(
    kernel, out_shape, n_in, us, scratch=(), smem_in=0, hbm_in=0, after=0, vmem_mib=24
):
    def body(*refs):
        n = smem_in + hbm_in + n_in
        kernel(*refs[:n], *refs[n + after :])

    vmem = pl.BlockSpec(memory_space=VM)
    return pl.pallas_call(
        body,
        out_shape=out_shape,
        in_specs=[pl.BlockSpec(memory_space=SM)] * smem_in
        + [pl.BlockSpec(memory_space=pltpu.HBM)] * hbm_in
        + [vmem] * n_in
        + [pl.BlockSpec(memory_space=pl.ANY)] * after,
        out_specs=jax.tree.map(lambda _: vmem, out_shape),
        scratch_shapes=list(scratch),
        compiler_params=pltpu.CompilerParams(vmem_limit_bytes=vmem_mib * 2**20),
        cost_estimate=pl.CostEstimate(
            flops=0, transcendentals=0, bytes_accessed=int(us * HBM_BYTES_PER_US)
        ),
    )


def doc_starts(lengths, pos):
    def step(n, carry):
        end, start = carry
        end = end + lengths[n]
        return end, jnp.where(pos >= end, end, start)

    return lax.fori_loop(0, 64, step, (jnp.int32(0), jnp.zeros_like(pos)))[1]


def prepare_kernel(info, lengths, q, w, q_heads, bias):
    core = info[0] % 2
    first = info[0] * TOK
    pos = first + lax.broadcasted_iota(jnp.int32, (1, TOK), 1)
    start = doc_starts(lengths, pos)
    for b, at in enumerate((0, -2, 2 * core - 3, -1 - 2 * core)):
        key_pos = first + at * TOK + lax.broadcasted_iota(jnp.int32, (TOK, 1), 0)
        ok = (key_pos >= start) & (key_pos <= pos)
        bias[b] = jnp.where(ok, 0.0, MASKED).astype(F32)
    for g in range(2):
        q_heads[g] = heads(q, g)


def heads(ref, g):
    return jnp.concatenate([ref[:, pl.ds((4 * g + h) * HD, HD)] for h in range(4)], axis=0)


def fwd_kernel(q, bias, own, two, mixed, swapped, att, lse, scores):
    refs = (own, two, mixed, swapped)
    for g in range(2):
        qg = q[g]
        top = jnp.full((1, 4 * TOK), MASKED, F32)
        for b, ref in enumerate(refs):
            s = dot_nt(ref[:, pl.ds(g * HD, HD)], qg) * EXP2_SCALE
            s = s + jnp.concatenate([bias[b]] * 4, axis=1)
            scores[b] = s
            top = jnp.maximum(top, jnp.max(s, axis=0, keepdims=True))
        total = jnp.zeros((1, 4 * TOK), F32)
        o = jnp.zeros((HD, 4 * TOK), F32)
        for b, ref in enumerate(refs):
            e = jnp.exp2(scores[b] - top)
            total = total + jnp.sum(e, axis=0, keepdims=True)
            o = o + dot_nn(ref[:, pl.ds((2 + g) * HD, HD)].T, e.astype(BF))
        lse[g : g + 1, :] = top + jnp.log2(total)
        o = (o / total).T
        for h in range(4):
            att[:, pl.ds((4 * g + h) * HD, HD)] = o[h * TOK : (h + 1) * TOK].astype(BF)


def bwd_kernel(
    q, bias, own, two, mixed, swapped, lse, att, attn_grad, dq, d_own, d_two, d_mixed, d_swapped
):
    refs = (own, two, mixed, swapped)
    outs = (d_own, d_two, d_mixed, d_swapped)
    for g in range(2):
        qg = q[g]
        og = heads(attn_grad, g)
        ag = heads(att, g)
        dots = jnp.sum((og.astype(F32) * ag.astype(F32)).T, axis=0, keepdims=True)
        row_lse = lse[g : g + 1, :]
        dqt = jnp.zeros((HD, 4 * TOK), F32)
        for b, (ref, out) in enumerate(zip(refs, outs)):
            kb = ref[:, pl.ds(g * HD, HD)]
            vb = ref[:, pl.ds((2 + g) * HD, HD)]
            s = dot_nt(kb, qg) * EXP2_SCALE + jnp.concatenate([bias[b]] * 4, axis=1)
            p = jnp.exp2(s - row_lse)
            out[:, pl.ds((2 + g) * HD, HD)] = dot_nn(p.astype(BF), og).astype(out.dtype)
            ds = (p * (dot_nt(vb, og) - dots) * SCALE).astype(BF)
            out[:, pl.ds(g * HD, HD)] = dot_nn(ds, qg).astype(out.dtype)
            dqt = dqt + dot_nn(kb.T, ds)
        dqs = dqt.T
        for h in range(4):
            dq[:, pl.ds((4 * g + h) * HD, HD)] = dqs[h * TOK : (h + 1) * TOK].astype(BF)


def finish_kernel(own, from_mixed, from_two, dk, dv, token):
    total = own[...] + from_mixed[...].astype(F32) + from_two[...].astype(F32)
    dk[...] = total[:, : 2 * HD].astype(BF)
    dv[...] = total[:, 2 * HD :].astype(BF)
    token[...] = jnp.zeros_like(token)


def layer_sum_kernel(own, from_opp, from_same, out, token):
    total = own[...] + from_opp[...].astype(F32) + from_same[...].astype(F32)
    out[...] = total.astype(BF)
    token[...] = jnp.zeros_like(token)


def chunk(ref, at, size):
    return ref[pl.ds(pl.multiple_of((at % SIDE) * size, size), size), :]


def out_first_kernel(info, att, w, across, opp):
    z, way = info[1], 1 - 2 * (info[0] % 2)
    rows = w.shape[0] // SIDE
    across[...] = dot_nt(att[...], chunk(w, z + 2, rows)).astype(BF)
    opp[...] = dot_nt(att[...], chunk(w, z + SIDE - way, rows)).astype(BF)


def out_second_kernel(info, att, w, relayed, same_out, own):
    z, way = info[1], 1 - 2 * (info[0] % 2)
    rows = w.shape[0] // SIDE
    term = dot_nt(att[...], chunk(w, z + SIDE + way, rows))
    same_out[...] = (term + relayed[...].astype(F32)).astype(BF)
    own[...] = dot_nt(att[...], chunk(w, z, rows))


def add_kernel(a, b, out):
    out[...] = (a[...] + b[...].astype(F32)).astype(BF)


def attn_grad_kernel(info, g, first, second, third, w, out):
    z, way = info[1], 1 - 2 * (info[0] % 2)
    rows = w.shape[0] // SIDE
    total = dot_nn(g[...], chunk(w, z, rows))
    total = total + dot_nn(first[...], chunk(w, z + SIDE - way, rows))
    total = total + dot_nn(second[...], chunk(w, z + SIDE + way, rows))
    total = total + dot_nn(third[...], chunk(w, z + 2, rows))
    out[...] = total.astype(BF)


def place(info):
    seq = info[0]
    core = seq % 2
    x, y = seq // (2 * SIDE), (seq // 2) % SIDE
    return core, jnp.where(core == 0, x, y), jnp.where(core == 0, y, x)


def weight_terms(info, g, a, outs):
    core, at, _ = place(info)

    @pl.when(core == 0)
    def _():
        for out, step in outs:
            out[...] = dot_nn(g[(at + step) % SIDE].T, a[...]).astype(out.dtype)

    @pl.when(core == 1)
    def _():
        for out, step in outs:
            strip = pl.ds(pl.multiple_of(((at + step) % SIDE) * TOK, TOK), TOK)
            for x in range(SIDE):
                terms = dot_nn(g[x, :, strip].T, a[...])
                out[x * TOK : (x + 1) * TOK, :] = terms.astype(out.dtype)


def weight_across_kernel(info, *refs):
    here, there, att, att_there, across, g, a = refs[:4], refs[4:8], *refs[8:]
    core, z = info[0] % 2, info[1]
    way = 1 - 2 * core
    half = a.shape[1]
    columns = pl.ds(pl.multiple_of(core * half, half), half)
    a[:TOK] = att[:, columns]
    a[TOK:] = att_there[:, columns]
    for t, sources, w in ((0, here, way), (1, there, -way)):
        for source, chunk_at in zip(sources, (z, z + SIDE - w, z + SIDE + w, z + 2)):
            g[chunk_at % SIDE, t * TOK : (t + 1) * TOK, :] = source[...]
    weight_terms(info, g, a, ((across, 2),))


def weight_next_kernel(info, g, a, plus, minus, own):
    weight_terms(info, g, a, ((plus, 1), (minus, SIDE - 1), (own, 0)))


def weight_sum_kernel(info, own, from_minus, from_plus, from_across, plus, minus, across, mine):
    core, _, at = place(info)
    for out, step in ((plus, 1), (minus, SIDE - 1), (across, 2), (mine, 0)):
        rows = pl.ds(pl.multiple_of(((at + step) % SIDE) * TOK, TOK), TOK)
        total = own[rows, :] + from_minus[rows, :].astype(F32) + from_plus[rows, :].astype(F32)
        out[...] = (total + from_across[rows, :].astype(F32)).astype(out.dtype)


def weight_halves_kernel(info, mine, a, b, c, keep, give):
    core = info[0] % 2
    for out, rows_of in ((keep, core), (give, 1 - core)):
        rows = pl.ds(pl.multiple_of(rows_of * HD, HD), HD)
        total = mine[rows, :] + a[rows, :].astype(F32) + b[rows, :].astype(F32)
        out[...] = (total + c[rows, :].astype(F32)).astype(BF)


def weight_join_kernel(info, kept, given, out):
    half = kept.shape[1]
    core = info[0] % 2
    out[:, pl.ds(pl.multiple_of(core * half, half), half)] = kept[...]
    out[:, pl.ds(pl.multiple_of((1 - core) * half, half), half)] = given[...]


def per_device(queries, keys, values, out_weight, out_grad, doc_lengths):
    shape = jax.ShapeDtypeStruct
    info = jnp.stack([lax.axis_index("seq"), lax.axis_index("kv")]).astype(jnp.int32)
    cols = queries.shape[1]
    half = cols // 2
    block = shape((TOK, cols), BF)

    own = jnp.pad(keys, ((0, 0), (0, 2 * HD))) + jnp.pad(values, ((0, 0), (2 * HD, 0)))
    two = seq_send(own, NEXT_CHIP)
    mixed = seq_send(own, MIXED)

    first = kv_send(out_grad, same)
    second = kv_send(lax.optimization_barrier((out_grad, own))[0], opposite)

    q, bias = call(
        prepare_kernel,
        [shape((2, 4 * TOK, HD), BF), shape((4, TOK, TOK), F32)],
        2,
        us=4,
        smem_in=2,
    )(info, doc_lengths, queries, out_weight)
    q, bias, mixed, two, first = lax.optimization_barrier((q, bias, mixed, two, first))
    swapped = seq_send(two, SWAP)
    blocks = (own, two, mixed, swapped)

    att, lse = call(
        fwd_kernel,
        [block, shape((2, 4 * TOK), F32)],
        6,
        us=4,
        scratch=[VM((4, TOK, 4 * TOK), F32)],
    )(q, bias, *blocks)
    third = kv_send(first, same)
    first, second, _ = lax.optimization_barrier((first, second, att))
    att_there = seq_send(att, SWAP)

    out_across, out_opp = call(out_first_kernel, [block] * 2, 2, us=2, smem_in=1)(info, att, out_weight)

    here = (out_grad, first, second, third)
    there = tuple(seq_send(v, SWAP) for v in (out_grad, first, second, third))
    pieces = shape((4 * TOK, half), BF)
    across, g, a = call(
        weight_across_kernel,
        [pieces, shape((SIDE, 2 * TOK, 4 * TOK), BF), shape((2 * TOK, half), BF)],
        10,
        us=4,
        smem_in=1,
        after=1,
    )(info, *here, *there, att, att_there, out_across)
    stage = ("x", "y")
    from_across = seq_send(across, by_core(stage, 2))
    plus, minus, weight_own = call(
        weight_next_kernel, [pieces] * 2 + [shape((4 * TOK, half), F32)], 2, us=4, smem_in=1
    )(info, g, a)
    from_minus = seq_send(plus, by_core(stage, 1))
    from_plus = seq_send(minus, by_core(stage, -1))

    send_across, send_opp, _ = lax.optimization_barrier((out_across, out_opp, plus))
    out_relayed = kv_send(send_across, same)
    out_from_opp = kv_send(send_opp, opposite)

    attn_grad = call(attn_grad_kernel, block, 5, us=3, smem_in=1, after=1)(
        info, *here, out_weight, plus
    )

    part = shape((TOK, 4 * HD), F32)
    part16 = shape((TOK, 4 * HD), BF)
    query_grad, d_own, d_two, d_mixed, d_swapped = call(
        bwd_kernel, [block, part, part, part16, part16], 9, us=6.5
    )(q, bias, *blocks, lse, att, attn_grad)
    from_swapped = seq_send(d_swapped, SWAP)
    from_mixed = seq_send(d_mixed, back(MIXED))
    out_same, out_own = call(
        out_second_kernel, [block, shape((TOK, cols), F32)], 3, us=2, smem_in=1, after=2
    )(info, att, out_weight, out_relayed, d_own, out_from_opp)
    d_two = call(add_kernel, part16, 2, us=1, after=2)(
        d_two, from_swapped, out_same, from_across
    )
    from_two = seq_send(d_two, back(NEXT_CHIP))
    out_from_same = kv_send(lax.optimization_barrier((out_same, d_two))[0], same)

    strip = shape((TOK, half), BF)
    plus, minus, across, mine = call(
        weight_sum_kernel,
        [strip] * 3 + [shape((TOK, half), F32)],
        4,
        us=1,
        smem_in=1,
        after=1,
    )(info, weight_own, from_minus, from_plus, from_across, d_two)
    stage = ("y", "x")
    last = [
        seq_send(across, by_core(stage, 2)),
        seq_send(plus, by_core(stage, 1)),
        seq_send(minus, by_core(stage, -1)),
    ]
    layer_out, token = call(layer_sum_kernel, [block, shape((8, HD), F32)], 3, us=1, after=1)(
        out_own, out_from_opp, out_from_same, across
    )
    key_grad, value_grad, token = call(
        finish_kernel, [shape((TOK, 2 * HD), BF)] * 2 + [shape((8, HD), F32)], 3, us=1, after=2
    )(d_own, from_mixed, from_two, token, last[0])
    kept, given = call(weight_halves_kernel, [shape((HD, half), BF)] * 2, 4, us=1, smem_in=1, after=1)(
        info, mine, *last, token
    )
    weight_grad = call(weight_join_kernel, shape((HD, cols), BF), 2, us=1, smem_in=1)(
        info, kept, seq_send(given, SWAP)
    )
    return (layer_out, query_grad, key_grad, value_grad, weight_grad)


def solution(mesh):
    placed = (P("seq", "kv"), P("seq", "kv"), P("seq", "kv"), P(None, "kv"), P("seq", "kv"), P())
    return jax.shard_map(
        per_device,
        mesh=mesh,
        in_specs=placed,
        out_specs=(P("seq", "kv"),) * 5,
        check_vma=False,
    )
```

```python
import math

import jax
import jax.numpy as jnp
from jax import lax
from jax.experimental import pallas as pl
from jax.experimental.pallas import tpu as pltpu
from jax.sharding import PartitionSpec as P

BF = jnp.bfloat16
F32 = jnp.float32
HD = 128
TOK = 256
SIDE = 4
SCALE = HD**-0.5
EXP2_SCALE = SCALE * math.log2(math.e)
MASKED = -1e30
HBM_BYTES_PER_US = 50_000
VM = pltpu.VMEM
SM = pltpu.SMEM


def dot_nn(a, b):
    return lax.dot_general(a, b, (((1,), (0,)), ((), ())), preferred_element_type=F32)


def dot_nt(a, b):
    return lax.dot_general(a, b, (((1,), (1,)), ((), ())), preferred_element_type=F32)


def seq_route(step):
    pairs = []
    for x in range(SIDE):
        for y in range(SIDE):
            for core in range(2):
                to = step(x, y, core)
                if to is not None:
                    pairs.append(((x * SIDE + y) * 2 + core, (to[0] * SIDE + to[1]) * 2 + to[2]))
    return pairs


def chips_on(x, y, chips, core):
    chip = (x * SIDE + y + chips) % (SIDE * SIDE)
    return (chip // SIDE, chip % SIDE, core)


SWAP = seq_route(lambda x, y, c: (x, y, 1 - c))
NEXT_CHIP = seq_route(lambda x, y, c: chips_on(x, y, 1, c))
MIXED = seq_route(lambda x, y, c: (x, y, 1) if c == 0 else chips_on(x, y, 2, 0))


def back(route):
    return [(b, a) for a, b in route]


def by_core(axis_of_core, step):
    def to(x, y, c):
        if axis_of_core[c] == "x":
            return ((x + step) % SIDE, y, c)
        return (x, (y + step) % SIDE, c)

    return seq_route(to)


def same(core):
    return 1 - 2 * core


def opposite(core):
    return 2 * core - 1


def seq_send(v, route):
    return lax.ppermute(v, "seq", route)


def kv_send(v, step):
    pairs = []
    for seq in range(2 * SIDE * SIDE):
        for z in range(SIDE):
            pairs.append((seq * SIDE + z, seq * SIDE + (z + step(seq % 2)) % SIDE))
    return lax.ppermute(v, ("seq", "kv"), pairs)


def call(
    kernel, out_shape, n_in, us, scratch=(), smem_in=0, hbm_in=0, after=0, vmem_mib=24
):
    def body(*refs):
        n = smem_in + hbm_in + n_in
        kernel(*refs[:n], *refs[n + after :])

    vmem = pl.BlockSpec(memory_space=VM)
    return pl.pallas_call(
        body,
        out_shape=out_shape,
        in_specs=[pl.BlockSpec(memory_space=SM)] * smem_in
        + [pl.BlockSpec(memory_space=pltpu.HBM)] * hbm_in
        + [vmem] * n_in
        + [pl.BlockSpec(memory_space=pl.ANY)] * after,
        out_specs=jax.tree.map(lambda _: vmem, out_shape),
        scratch_shapes=list(scratch),
        compiler_params=pltpu.CompilerParams(vmem_limit_bytes=vmem_mib * 2**20),
        cost_estimate=pl.CostEstimate(
            flops=0, transcendentals=0, bytes_accessed=int(us * HBM_BYTES_PER_US)
        ),
    )


def doc_starts(lengths, pos):
    def step(n, carry):
        end, start = carry
        end = end + lengths[n]
        return end, jnp.where(pos >= end, end, start)

    return lax.fori_loop(0, 64, step, (jnp.int32(0), jnp.zeros_like(pos)))[1]


def prepare_kernel(info, lengths, q, w, q_heads, bias):
    core = info[0] % 2
    first = info[0] * TOK
    pos = first + lax.broadcasted_iota(jnp.int32, (1, TOK), 1)
    start = doc_starts(lengths, pos)
    for b, at in enumerate((0, -2, 2 * core - 3, -1 - 2 * core)):
        key_pos = first + at * TOK + lax.broadcasted_iota(jnp.int32, (TOK, 1), 0)
        ok = (key_pos >= start) & (key_pos <= pos)
        bias[b] = jnp.where(ok, 0.0, MASKED).astype(F32)
    for g in range(2):
        q_heads[g] = heads(q, g)


def heads(ref, g):
    return jnp.concatenate([ref[:, pl.ds((4 * g + h) * HD, HD)] for h in range(4)], axis=0)


def fwd_kernel(q, bias, own, two, mixed, swapped, att, lse, scores):
    refs = (own, two, mixed, swapped)
    for g in range(2):
        qg = q[g]
        top = jnp.full((1, 4 * TOK), MASKED, F32)
        for b, ref in enumerate(refs):
            s = dot_nt(ref[:, pl.ds(g * HD, HD)], qg) * EXP2_SCALE
            s = s + jnp.concatenate([bias[b]] * 4, axis=1)
            scores[b] = s
            top = jnp.maximum(top, jnp.max(s, axis=0, keepdims=True))
        total = jnp.zeros((1, 4 * TOK), F32)
        o = jnp.zeros((HD, 4 * TOK), F32)
        for b, ref in enumerate(refs):
            e = jnp.exp2(scores[b] - top)
            total = total + jnp.sum(e, axis=0, keepdims=True)
            o = o + dot_nn(ref[:, pl.ds((2 + g) * HD, HD)].T, e.astype(BF))
        lse[g : g + 1, :] = top + jnp.log2(total)
        o = (o / total).T
        for h in range(4):
            att[:, pl.ds((4 * g + h) * HD, HD)] = o[h * TOK : (h + 1) * TOK].astype(BF)


def bwd_kernel(
    q, bias, own, two, mixed, swapped, lse, att, attn_grad, dq, d_own, d_two, d_mixed, d_swapped
):
    refs = (own, two, mixed, swapped)
    outs = (d_own, d_two, d_mixed, d_swapped)
    for g in range(2):
        qg = q[g]
        og = heads(attn_grad, g)
        ag = heads(att, g)
        dots = jnp.sum((og.astype(F32) * ag.astype(F32)).T, axis=0, keepdims=True)
        row_lse = lse[g : g + 1, :]
        dqt = jnp.zeros((HD, 4 * TOK), F32)
        for b, (ref, out) in enumerate(zip(refs, outs)):
            kb = ref[:, pl.ds(g * HD, HD)]
            vb = ref[:, pl.ds((2 + g) * HD, HD)]
            s = dot_nt(kb, qg) * EXP2_SCALE + jnp.concatenate([bias[b]] * 4, axis=1)
            p = jnp.exp2(s - row_lse)
            out[:, pl.ds((2 + g) * HD, HD)] = dot_nn(p.astype(BF), og).astype(out.dtype)
            ds = (p * (dot_nt(vb, og) - dots) * SCALE).astype(BF)
            out[:, pl.ds(g * HD, HD)] = dot_nn(ds, qg).astype(out.dtype)
            dqt = dqt + dot_nn(kb.T, ds)
        dqs = dqt.T
        for h in range(4):
            dq[:, pl.ds((4 * g + h) * HD, HD)] = dqs[h * TOK : (h + 1) * TOK].astype(BF)


def finish_kernel(own, from_mixed, from_two, dk, dv, token):
    total = own[...] + from_mixed[...].astype(F32) + from_two[...].astype(F32)
    dk[...] = total[:, : 2 * HD].astype(BF)
    dv[...] = total[:, 2 * HD :].astype(BF)
    token[...] = jnp.zeros_like(token)


def layer_sum_kernel(own, from_opp, from_same, out, token):
    total = own[...] + from_opp[...].astype(F32) + from_same[...].astype(F32)
    out[...] = total.astype(BF)
    token[...] = jnp.zeros_like(token)


def chunk(ref, at, size):
    return ref[pl.ds(pl.multiple_of((at % SIDE) * size, size), size), :]


def out_first_kernel(info, att, w, across, opp):
    z, way = info[1], 1 - 2 * (info[0] % 2)
    rows = w.shape[0] // SIDE
    across[...] = dot_nt(att[...], chunk(w, z + 2, rows)).astype(BF)
    opp[...] = dot_nt(att[...], chunk(w, z + SIDE - way, rows)).astype(BF)


def out_second_kernel(info, att, w, relayed, same_out, own):
    z, way = info[1], 1 - 2 * (info[0] % 2)
    rows = w.shape[0] // SIDE
    term = dot_nt(att[...], chunk(w, z + SIDE + way, rows))
    same_out[...] = (term + relayed[...].astype(F32)).astype(BF)
    own[...] = dot_nt(att[...], chunk(w, z, rows))


def add_kernel(a, b, out):
    out[...] = (a[...] + b[...].astype(F32)).astype(BF)


def attn_grad_kernel(info, g, first, second, third, w, out):
    z, way = info[1], 1 - 2 * (info[0] % 2)
    rows = w.shape[0] // SIDE
    total = dot_nn(g[...], chunk(w, z, rows))
    total = total + dot_nn(first[...], chunk(w, z + SIDE - way, rows))
    total = total + dot_nn(second[...], chunk(w, z + SIDE + way, rows))
    total = total + dot_nn(third[...], chunk(w, z + 2, rows))
    out[...] = total.astype(BF)


def place(info):
    seq = info[0]
    core = seq % 2
    x, y = seq // (2 * SIDE), (seq // 2) % SIDE
    return core, jnp.where(core == 0, x, y), jnp.where(core == 0, y, x)


def weight_terms(info, g, a, outs):
    core, at, _ = place(info)

    @pl.when(core == 0)
    def _():
        for out, step in outs:
            out[...] = dot_nn(g[(at + step) % SIDE].T, a[...]).astype(out.dtype)

    @pl.when(core == 1)
    def _():
        for out, step in outs:
            strip = pl.ds(pl.multiple_of(((at + step) % SIDE) * TOK, TOK), TOK)
            for x in range(SIDE):
                terms = dot_nn(g[x, :, strip].T, a[...])
                out[x * TOK : (x + 1) * TOK, :] = terms.astype(out.dtype)


def weight_across_kernel(info, *refs):
    here, there, att, att_there, across, g, a = refs[:4], refs[4:8], *refs[8:]
    core, z = info[0] % 2, info[1]
    way = 1 - 2 * core
    half = a.shape[1]
    columns = pl.ds(pl.multiple_of(core * half, half), half)
    a[:TOK] = att[:, columns]
    a[TOK:] = att_there[:, columns]
    for t, sources, w in ((0, here, way), (1, there, -way)):
        for source, chunk_at in zip(sources, (z, z + SIDE - w, z + SIDE + w, z + 2)):
            g[chunk_at % SIDE, t * TOK : (t + 1) * TOK, :] = source[...]
    weight_terms(info, g, a, ((across, 2),))


def weight_next_kernel(info, g, a, plus, minus):
    weight_terms(info, g, a, ((plus, 1), (minus, SIDE - 1)))


def weight_own_kernel(info, g, a, own):
    weight_terms(info, g, a, ((own, 0),))


def weight_sum_kernel(info, own, from_minus, from_plus, from_across, plus, minus, across, mine):
    core, _, at = place(info)
    for out, step in ((plus, 1), (minus, SIDE - 1), (across, 2), (mine, 0)):
        rows = pl.ds(pl.multiple_of(((at + step) % SIDE) * TOK, TOK), TOK)
        total = own[rows, :] + from_minus[rows, :].astype(F32) + from_plus[rows, :].astype(F32)
        out[...] = (total + from_across[rows, :].astype(F32)).astype(out.dtype)


def weight_halves_kernel(info, mine, a, b, c, keep, give):
    core = info[0] % 2
    for out, rows_of in ((keep, core), (give, 1 - core)):
        rows = pl.ds(pl.multiple_of(rows_of * HD, HD), HD)
        total = mine[rows, :] + a[rows, :].astype(F32) + b[rows, :].astype(F32)
        out[...] = (total + c[rows, :].astype(F32)).astype(BF)


def weight_join_kernel(info, kept, given, out):
    half = kept.shape[1]
    core = info[0] % 2
    out[:, pl.ds(pl.multiple_of(core * half, half), half)] = kept[...]
    out[:, pl.ds(pl.multiple_of((1 - core) * half, half), half)] = given[...]


def per_device(queries, keys, values, out_weight, out_grad, doc_lengths):
    shape = jax.ShapeDtypeStruct
    info = jnp.stack([lax.axis_index("seq"), lax.axis_index("kv")]).astype(jnp.int32)
    cols = queries.shape[1]
    half = cols // 2
    block = shape((TOK, cols), BF)

    own = jnp.pad(keys, ((0, 0), (0, 2 * HD))) + jnp.pad(values, ((0, 0), (2 * HD, 0)))
    two = seq_send(own, NEXT_CHIP)
    mixed = seq_send(own, MIXED)

    first = kv_send(out_grad, same)
    second = kv_send(lax.optimization_barrier((out_grad, own))[0], opposite)

    q, bias = call(
        prepare_kernel,
        [shape((2, 4 * TOK, HD), BF), shape((4, TOK, TOK), F32)],
        2,
        us=4,
        smem_in=2,
    )(info, doc_lengths, queries, out_weight)
    q, bias, mixed, two, first = lax.optimization_barrier((q, bias, mixed, two, first))
    swapped = seq_send(two, SWAP)
    blocks = (own, two, mixed, swapped)

    att, lse = call(
        fwd_kernel,
        [block, shape((2, 4 * TOK), F32)],
        6,
        us=4,
        scratch=[VM((4, TOK, 4 * TOK), F32)],
    )(q, bias, *blocks)
    third = kv_send(first, same)
    first, second, _ = lax.optimization_barrier((first, second, att))
    att_there = seq_send(att, SWAP)

    out_across, out_opp = call(out_first_kernel, [block] * 2, 2, us=2, smem_in=1)(info, att, out_weight)

    here = (out_grad, first, second, third)
    there = tuple(seq_send(v, SWAP) for v in (out_grad, first, second, third))
    pieces = shape((4 * TOK, half), BF)
    across, g, a = call(
        weight_across_kernel,
        [pieces, shape((SIDE, 2 * TOK, 4 * TOK), BF), shape((2 * TOK, half), BF)],
        10,
        us=4,
        smem_in=1,
        after=1,
    )(info, *here, *there, att, att_there, out_across)
    stage = ("x", "y")
    from_across = seq_send(across, by_core(stage, 2))
    plus, minus = call(weight_next_kernel, [pieces] * 2, 2, us=4, smem_in=1)(info, g, a)
    from_minus = seq_send(plus, by_core(stage, 1))
    from_plus = seq_send(minus, by_core(stage, -1))

    send_across, send_opp, _ = lax.optimization_barrier((out_across, out_opp, plus))
    out_relayed = kv_send(send_across, same)
    out_from_opp = kv_send(send_opp, opposite)

    attn_grad = call(attn_grad_kernel, block, 5, us=3, smem_in=1, after=1)(
        info, *here, out_weight, plus
    )

    part = shape((TOK, 4 * HD), F32)
    part16 = shape((TOK, 4 * HD), BF)
    query_grad, d_own, d_two, d_mixed, d_swapped = call(
        bwd_kernel, [block, part, part, part16, part16], 9, us=6.5
    )(q, bias, *blocks, lse, att, attn_grad)
    from_swapped = seq_send(d_swapped, SWAP)
    from_mixed = seq_send(d_mixed, back(MIXED))
    out_same, out_own = call(
        out_second_kernel, [block, shape((TOK, cols), F32)], 3, us=2, smem_in=1, after=2
    )(info, att, out_weight, out_relayed, d_own, out_from_opp)
    d_two = call(add_kernel, part16, 2, us=1, after=2)(
        d_two, from_swapped, out_same, from_across
    )
    from_two = seq_send(d_two, back(NEXT_CHIP))
    out_from_same = kv_send(lax.optimization_barrier((out_same, d_two))[0], same)

    weight_own = call(weight_own_kernel, shape((4 * TOK, half), F32), 2, us=1, smem_in=1, after=1)(
        info, g, a, d_two
    )
    strip = shape((TOK, half), BF)
    plus, minus, across, mine = call(
        weight_sum_kernel,
        [strip] * 3 + [shape((TOK, half), F32)],
        4,
        us=1,
        smem_in=1,
        after=1,
    )(info, weight_own, from_minus, from_plus, from_across, d_two)
    stage = ("y", "x")
    last = [
        seq_send(across, by_core(stage, 2)),
        seq_send(plus, by_core(stage, 1)),
        seq_send(minus, by_core(stage, -1)),
    ]
    layer_out, token = call(layer_sum_kernel, [block, shape((8, HD), F32)], 3, us=1, after=1)(
        out_own, out_from_opp, out_from_same, across
    )
    key_grad, value_grad, token = call(
        finish_kernel, [shape((TOK, 2 * HD), BF)] * 2 + [shape((8, HD), F32)], 3, us=1, after=2
    )(d_own, from_mixed, from_two, token, last[0])
    kept, given = call(weight_halves_kernel, [shape((HD, half), BF)] * 2, 4, us=1, smem_in=1, after=1)(
        info, mine, *last, token
    )
    weight_grad = call(weight_join_kernel, shape((HD, cols), BF), 2, us=1, smem_in=1)(
        info, kept, seq_send(given, SWAP)
    )
    return (layer_out, query_grad, key_grad, value_grad, weight_grad)


def solution(mesh):
    placed = (P("seq", "kv"), P("seq", "kv"), P("seq", "kv"), P(None, "kv"), P("seq", "kv"), P())
    return jax.shard_map(
        per_device,
        mesh=mesh,
        in_specs=placed,
        out_specs=(P("seq", "kv"),) * 5,
        check_vma=False,
    )
```
